256 devices in a mesh: cuts: 2 (over y_hi), blk: 128 (over z, y_lo, x, core).
Axes of the slice: x: 4, y: 4 (y_hi: 2, y_lo: 2; y = y_hi * 2 + y_lo), z: 8, core: 2. Of those that a mesh axis runs over, the one named last changes fastest.
Arguments:
- image_embed: float32 [32768, 1152], P(('cuts', 'blk')), may hold values from -0.1875 to 0.1875
- text_embed: float32 [32768, 1152], P(('cuts', 'blk')), may hold values from -0.1875 to 0.1875
- log_scale: float32 [1], replicated, may hold values from 0.5 to 2.3
- bias: float32 [1], replicated, may hold values from -4 to -1
Outputs:
- image_grad: float32 [32768, 1152], P(('cuts', 'blk'))
- text_grad: float32 [32768, 1152], P(('cuts', 'blk'))
The draws below stay inside these ranges and needn't reach their ends.
All inputs are finite; a program needn't handle non-finite values.
Results may differ from the reference program's by a relative error of at most 0.0003.
Values sent between devices are 32-bit elements; how exact they have to be, the bound alone decides.
No kernel may reach another device: no remote copies, remote signals or barrier semaphores. Data moves between devices by JAX's collectives and lax.ppermute only.
A program may use at most 128 MiB of HBM per device.

```python
import jax
import jax.numpy as jnp
from jax import lax

D = 1152
ROWS = 128
STEPS = 8
BATCH = 32768
N_CUTS = 2
N_BLK = 128


def block_levels(key, dims, shards, smallest, high):
    level, own = 1.0, jax.random.fold_in(key, 6)
    for axis_at, blocks in shards:
        heights = jnp.exp(jax.random.uniform(jax.random.fold_in(own, axis_at), (blocks,), jnp.float32, smallest / len(shards), high / len(shards)))
        level = level * jnp.repeat(heights, dims[axis_at] // blocks).reshape([-1 if axis == axis_at else 1 for axis in range(len(dims))])
    return level


def centred(key, shape, spread, limit, cuts=(), held_as=jnp.bfloat16):
    level = block_levels(key, shape, cuts, -0.22, 0.18) if cuts else 1.0
    values = jax.random.normal(key, shape, jnp.float32) * spread * level
    return jnp.minimum(jnp.maximum(values, -limit), limit).astype(held_as)


def setup_inputs(seed: int = 0) -> dict:
    arg_keys = jax.random.split(jax.random.key(seed), 5)
    image_embed = centred(arg_keys[0], (BATCH, D), (D ** -0.5), 0.1875, ((0, 256),), jnp.float32)
    text_embed = centred(arg_keys[1], (BATCH, D), (D ** -0.5), 0.1875, ((0, 256),), jnp.float32)
    log_scale = jnp.clip(jax.random.uniform(arg_keys[2], (1,), jnp.float32, 0.5, 2.3), 0.5, 2.3)
    bias = jnp.clip(jax.random.uniform(arg_keys[3], (1,), jnp.float32, -4.0, -1.0), -4.0, -1.0)
    return {"image_embed": image_embed, "text_embed": text_embed, "log_scale": log_scale, "bias": bias}


def normalize(rows_in):
    inverse = lax.rsqrt(lax.optimization_barrier(jnp.sum(rows_in * rows_in, axis=-1, keepdims=True)) + 1e-06)
    return (rows_in * inverse, inverse)

def pair_grad(logits, positive):
    signs = jnp.where(positive, jnp.float32(1.0), jnp.float32(-1.0))
    return -signs * jax.nn.sigmoid(-signs * logits)

def reference(image_embed, text_embed, log_scale, bias):
    x_rows, x_inv = normalize(image_embed)
    y_rows, y_inv = normalize(text_embed)
    scale = jnp.exp(log_scale[0])
    shift_bias = bias[0]
    blocks = N_CUTS * N_BLK
    x_blocks = x_rows.reshape(blocks, ROWS, D)
    y_blocks = y_rows.reshape(blocks, ROWS, D)
    diagonal = jnp.eye(ROWS, dtype=bool)
    hp = lax.Precision.HIGHEST

    def image_block(q_index):
        group = q_index // N_BLK
        place = q_index % N_BLK
        x_here = x_blocks[q_index]
        total = jnp.zeros((ROWS, D), jnp.float32)
        for step in range(STEPS):
            for other in range(N_CUTS):
                p_index = (other * N_BLK + (place - step) % N_BLK).astype(jnp.int32)
                y_there = y_blocks[p_index]
                logits = scale * jnp.dot(x_here, y_there.T, precision=hp) + shift_bias
                positive = diagonal & (step == 0) & (other == group)
                grads = pair_grad(logits, positive)
                total = total + jnp.dot(grads, y_there, precision=hp)
        return scale * total

    def text_block(p_index):
        group = p_index // N_BLK
        place = p_index % N_BLK
        y_here = y_blocks[p_index]
        total = jnp.zeros((ROWS, D), jnp.float32)
        for step in range(STEPS):
            for other in range(N_CUTS):
                q_index = (other * N_BLK + (place + step) % N_BLK).astype(jnp.int32)
                x_there = x_blocks[q_index]
                logits = scale * jnp.dot(x_there, y_here.T, precision=hp) + shift_bias
                positive = diagonal & (step == 0) & (other == group)
                grads = pair_grad(logits, positive)
                total = total + jnp.dot(grads.T, x_there, precision=hp)
        return scale * total
    image_part = lax.map(image_block, jnp.arange(blocks, dtype=jnp.int32)).reshape(BATCH, D)
    text_part = lax.map(text_block, jnp.arange(blocks, dtype=jnp.int32)).reshape(BATCH, D)
    image_grad = x_inv * (image_part - x_rows * lax.optimization_barrier(jnp.sum(x_rows * image_part, axis=-1, keepdims=True)))
    text_grad = y_inv * (text_part - y_rows * lax.optimization_barrier(jnp.sum(y_rows * text_part, axis=-1, keepdims=True)))
    return (image_grad, text_grad)
```

```python
import jax
import jax.numpy as jnp
from jax import lax
from jax.sharding import PartitionSpec as P

GROUPS, BLOCKS = 2, 128
HIGH = lax.Precision.HIGH


def moved(block, place):
    pairs = []
    for group in range(GROUPS):
        for position in range(BLOCKS):
            to_group, to_position = place(group, position)
            pairs.append((group * BLOCKS + position, to_group * BLOCKS + to_position % BLOCKS))
    return lax.ppermute(block, ("cuts", "blk"), pairs)


def along(distance):
    return lambda group, position: (group, position + distance)


def other_core(group, position):
    return group, position ^ 1


def other_group(group, position):
    return 1 - group, position


def odd_along(distance):
    return lambda group, position: (group, position + distance * (position % 2))


def normalize(rows_in):
    inverse = lax.rsqrt(jnp.sum(rows_in * rows_in, axis=-1, keepdims=True) + 1e-06)
    return (rows_in * inverse, inverse)


def local(image_embed, text_embed, log_scale, bias):
    x_own, x_inv = normalize(image_embed)
    y_own, y_inv = normalize(text_embed)
    scale = jnp.exp(log_scale[0])
    shift = bias[0]
    rows = x_own.shape[0]
    y_far = [moved(y_own, along(2 * d)) for d in (1, 2, 3)]
    x_cut = moved(x_own, other_group)
    y_alt = moved(y_own, odd_along(8))
    x_here = jnp.concatenate([x_own, x_cut])
    x_near = moved(x_here, other_core)
    x_all = jnp.concatenate([x_here, x_near])

    def pair_terms(x_rows, y_rows, own):
        logits = scale * jnp.dot(x_rows, y_rows.T, precision=HIGH) + shift
        if own:
            row_ids = lax.broadcasted_iota(jnp.int32, logits.shape, 0)
            col_ids = lax.broadcasted_iota(jnp.int32, logits.shape, 1)
            positive = row_ids == col_ids
            signed = jax.nn.sigmoid(jnp.where(positive, -logits, logits))
            grads = jnp.where(positive, -signed, signed)
        else:
            grads = jax.nn.sigmoid(logits)
        to_image = jnp.dot(grads, y_rows, precision=HIGH)
        to_text = jnp.dot(grads.T, x_rows, precision=HIGH)
        return to_image, to_text

    gx_here, gy_own = pair_terms(x_here, y_own, True)
    gx_near, gy_alt = pair_terms(x_near, y_alt, False)
    gx_all = jnp.concatenate([gx_here, gx_near])
    for d, y_rows in zip((1, 2, 3), y_far):
        to_image, to_text = pair_terms(x_all, y_rows, False)
        gx_all = gx_all + to_image
        gy_own = gy_own + moved(to_text, along(-2 * d))
    gy_own = gy_own + moved(gy_alt, odd_along(-8))
    gx = gx_all[: 2 * rows] + moved(gx_all[2 * rows :], other_core)
    gx_own = gx[:rows] + moved(gx[rows:], other_group)
    image_part = scale * gx_own
    text_part = scale * gy_own
    image_grad = x_inv * (image_part - x_own * jnp.sum(x_own * image_part, axis=-1, keepdims=True))
    text_grad = y_inv * (text_part - y_own * jnp.sum(y_own * text_part, axis=-1, keepdims=True))
    return (image_grad, text_grad)


def solution(mesh):
    rows = P(("cuts", "blk"), None)
    return jax.shard_map(
        local, mesh=mesh, in_specs=(rows, rows, P(), P()), out_specs=(rows, rows), check_vma=False
    )
```

```python
import jax
import jax.numpy as jnp
from jax import lax
from jax.sharding import PartitionSpec as P

GROUPS, BLOCKS, ROW = 2, 128, 8
HIGH = lax.Precision.HIGH


def moved(block, place):
    pairs = []
    for group in range(GROUPS):
        for position in range(BLOCKS):
            to_group, to_position = place(group, position)
            pairs.append((group * BLOCKS + position, to_group * BLOCKS + to_position % BLOCKS))
    return lax.ppermute(block, ("cuts", "blk"), pairs)


def next_row(group, position):
    return (group, position + ROW) if position % 2 == 0 else (1 - group, position + ROW)


def last_row(group, position):
    return (group, position - ROW) if position % 2 == 0 else (1 - group, position - ROW)


def in_row(chips):
    return lambda group, position: (
        group,
        position // ROW * ROW + (position + 2 * chips) % ROW,
    )


def other_core(group, position):
    return group, position ^ 1


def other_group(group, position):
    return 1 - group, position


def normalize(rows_in):
    inverse = lax.rsqrt(jnp.sum(rows_in * rows_in, axis=-1, keepdims=True) + 1e-06)
    return (rows_in * inverse, inverse)


def local(image_embed, text_embed, log_scale, bias):
    x_own, x_inv = normalize(image_embed)
    y_own, y_inv = normalize(text_embed)
    scale = jnp.exp(log_scale[0])
    shift = bias[0]
    rows = x_own.shape[0]
    position = lax.axis_index("blk")
    column = position % ROW // 2
    odd = position % 2 == 1
    y_last = moved(y_own, next_row)
    hops = (1, 2, -1)
    from_last = [column >= 3, column >= 2, column >= 1]
    y_far = [
        moved(jnp.where(last, y_last, y_own), in_row(hop)) for hop, last in zip(hops, from_last)
    ]
    x_cut = moved(x_own, other_group)
    y_alt = jnp.where(odd, y_last, y_own)
    x_here = jnp.concatenate([x_own, x_cut])
    x_near = moved(x_here, other_core)
    x_all = jnp.concatenate([x_here, x_near])

    def pair_terms(x_rows, y_rows, own):
        logits = scale * jnp.dot(x_rows, y_rows.T, precision=HIGH) + shift
        if own:
            row_ids = lax.broadcasted_iota(jnp.int32, logits.shape, 0)
            col_ids = lax.broadcasted_iota(jnp.int32, logits.shape, 1)
            positive = row_ids == col_ids
            signed = jax.nn.sigmoid(jnp.where(positive, -logits, logits))
            grads = jnp.where(positive, -signed, signed)
        else:
            grads = jax.nn.sigmoid(logits)
        to_image = jnp.dot(grads, y_rows, precision=HIGH)
        to_text = jnp.dot(grads.T, x_rows, precision=HIGH)
        return to_image, to_text

    gx_here, gy_own = pair_terms(x_here, y_own, True)
    gx_near, gy_alt = pair_terms(x_near, y_alt, False)
    gx_all = jnp.concatenate([gx_here, gx_near])
    gy_last = jnp.where(odd, gy_alt, 0.0)
    gy_own = gy_own + jnp.where(odd, 0.0, gy_alt)
    for hop, last, y_rows in zip(hops, from_last, y_far):
        to_image, to_text = pair_terms(x_all, y_rows, False)
        gx_all = gx_all + to_image
        back = moved(to_text, in_row(-hop))
        gy_last = gy_last + jnp.where(last, back, 0.0)
        gy_own = gy_own + jnp.where(last, 0.0, back)
    gy_own = gy_own + moved(gy_last, last_row)
    gx = gx_all[: 2 * rows] + moved(gx_all[2 * rows :], other_core)
    gx_own = gx[:rows] + moved(gx[rows:], other_group)
    image_part = scale * gx_own
    text_part = scale * gy_own
    image_grad = x_inv * (image_part - x_own * jnp.sum(x_own * image_part, axis=-1, keepdims=True))
    text_grad = y_inv * (text_part - y_own * jnp.sum(y_own * text_part, axis=-1, keepdims=True))
    return (image_grad, text_grad)


def solution(mesh):
    rows = P(("cuts", "blk"), None)
    return jax.shard_map(
        local, mesh=mesh, in_specs=(rows, rows, P(), P()), out_specs=(rows, rows), check_vma=False
    )
```

```python
import jax
import jax.numpy as jnp
from jax import lax
from jax.experimental import pallas as pl
from jax.experimental.pallas import tpu as pltpu
from jax.sharding import PartitionSpec as P

GROUPS, BLOCKS, ROW = 2, 128, 8
WEIGHT = 40_000_000


def moved(block, place):
    pairs = []
    for group in range(GROUPS):
        for position in range(BLOCKS):
            to_group, to_position = place(group, position)
            pairs.append((group * BLOCKS + position, to_group * BLOCKS + to_position % BLOCKS))
    return lax.ppermute(block, ("cuts", "blk"), pairs)


def next_row(group, position):
    return (group, position + ROW) if position % 2 == 0 else (1 - group, position + ROW)


def last_row(group, position):
    return (group, position - ROW) if position % 2 == 0 else (1 - group, position - ROW)


def in_row(chips):
    return lambda group, position: (
        group,
        position // ROW * ROW + (position + 2 * chips) % ROW,
    )


def other_core(group, position):
    return group, position ^ 1


def other_group(group, position):
    return 1 - group, position


def together(*values):
    return lax.optimization_barrier(values)


def split(values):
    high = values.astype(jnp.bfloat16)
    return high, (values - high.astype(jnp.float32)).astype(jnp.bfloat16)


def dot3(a, b, b_dim):
    dims = (((1,), (b_dim,)), ((), ()))
    (a_high, a_low), (b_high, b_low) = a, b

    def one(u, v):
        return lax.dot_general(u, v, dims, preferred_element_type=jnp.float32)

    return one(a_high, b_high) + (one(a_low, b_high) + one(a_high, b_low))


def sigmoid(values):
    return 1.0 / (1.0 + jnp.exp(-values))


def normalize_kernel(in_ref, out_ref, inverse_ref, *halves):
    values = in_ref[...]
    inverse = lax.rsqrt(jnp.sum(values * values, axis=-1, keepdims=True) + 1e-06)
    inverse_ref[...] = inverse
    values = values * inverse
    out_ref[...] = values
    for at, half in enumerate(halves):
        half[...] = values[at * half.shape[0] : (at + 1) * half.shape[0], :]


def far_kernel(params, *refs):
    images, (y_1, y_3, y_2) = refs[:6], refs[6:9]
    high_ref, low_ref, grads_ref, *outs = refs[9:]
    rows = y_1.shape[0]
    at = 0
    for image in images:
        high, low = split(image[...])
        high_ref[at : at + image.shape[0], :] = high
        low_ref[at : at + image.shape[0], :] = low
        at += image.shape[0]
    image = (high_ref[...], low_ref[...])
    text = split(jnp.concatenate([y_1[...], y_3[...], y_2[...]], axis=0))
    grads = sigmoid(params[0] * dot3(text, image, 1) + params[1])
    grads_ref[...] = grads
    to_text = dot3(split(grads), image, 0)
    for at, out in enumerate(outs):
        out[...] = to_text[at * rows : (at + 1) * rows, :]


def near_kernel(params, places, *refs):
    (own, last, y_1, y_3, y_2, high_ref, low_ref, far_grads_ref), outs = refs[:8], refs[8:]
    double = high_ref.shape[0] // 2
    far = split(jnp.concatenate([y_1[...], y_3[...], y_2[...]], axis=0))
    for side, mine, other, to_text in ((0, *outs[:3]), (1, *outs[3:])):
        at = side * double
        image = (high_ref[at : at + double, :], low_ref[at : at + double, :])
        text = own[...]
        if side == 1:
            text = jnp.where(places[0] == 1, last[...], text)
        text = split(text)
        logits = params[0] * dot3(text, image, 1) + params[1]
        if side == 0:
            row_ids = lax.broadcasted_iota(jnp.int32, logits.shape, 0)
            col_ids = lax.broadcasted_iota(jnp.int32, logits.shape, 1)
            signs = jnp.where(row_ids == col_ids, -1.0, 1.0)
            grads = signs * sigmoid(signs * logits)
        else:
            grads = sigmoid(logits)
        to_text[...] = dot3(split(grads), image, 0)
        all_grads = jnp.concatenate([far_grads_ref[:, at : at + double], grads], axis=0)
        all_text = tuple(jnp.concatenate(parts, axis=0) for parts in zip(far, text))
        to_image = dot3(split(all_grads.T), all_text, 0)
        mine[...] = to_image[: double // 2, :]
        other[...] = to_image[double // 2 :, :]


def select_kernel(places, own, last, one_ref, three_ref):
    one_ref[...] = jnp.where(places[2] == 1, last[...], own[...])
    three_ref[...] = jnp.where(places[3] == 1, last[...], own[...])


def select_two_kernel(places, two, two_last, out_ref):
    out_ref[...] = jnp.where(places[1] == 1, two_last[...], two[...])


def last_kernel(places, near, back_1, back_3, out_ref):
    total = jnp.where(places[0] == 1, near[...], 0.0)
    total = total + jnp.where(places[2] == 1, back_1[...], 0.0)
    out_ref[...] = total + jnp.where(places[3] == 1, back_3[...], 0.0)


def own_kernel(places, here, near, back_1, back_3, out_ref):
    total = here[...] + jnp.where(places[0] == 1, 0.0, near[...])
    total = total + jnp.where(places[2] == 1, 0.0, back_1[...])
    out_ref[...] = total + jnp.where(places[3] == 1, 0.0, back_3[...])


def add_kernel(here, beside, *halves):
    total = here[...] + beside[...]
    for at, half in enumerate(halves):
        half[...] = total[at * half.shape[0] : (at + 1) * half.shape[0], :]


def finish_kernel(params, rows_ref, inverse_ref, *refs):
    *parts, out_ref = refs
    rows = rows_ref[...]
    count = rows.shape[0]
    halves = [part[...] for part in parts if part.shape[0] < count]
    total = sum(part[...] for part in parts if part.shape[0] == count)
    if halves:
        total = total + jnp.concatenate(halves, axis=0)
    total = params[0] * total
    along = jnp.sum(rows * total, axis=-1, keepdims=True)
    out_ref[...] = inverse_ref[...] * (total - rows * along)


def call(kernel, outs, scalars, *arrays, out_memory=pltpu.VMEM, weight=0):
    vmem = pl.BlockSpec(memory_space=pltpu.VMEM)
    smem = pl.BlockSpec(memory_space=pltpu.SMEM)
    result = pl.BlockSpec(memory_space=out_memory) if out_memory else pl.BlockSpec()
    return pl.pallas_call(
        kernel,
        out_shape=[jax.ShapeDtypeStruct(shape, dtype) for shape, dtype in outs],
        in_specs=[smem] * len(scalars) + [vmem] * len(arrays),
        out_specs=[result] * len(outs),
        compiler_params=pltpu.CompilerParams(vmem_limit_bytes=16 * 2**20),
        cost_estimate=pl.CostEstimate(flops=0, transcendentals=0, bytes_accessed=weight),
    )(*scalars, *arrays)


def normalize(rows_in, halves=0):
    rows, width = rows_in.shape
    outs = [((rows, width), jnp.float32), ((rows, 1), jnp.float32)]
    outs += [((rows // 2, width), jnp.float32)] * halves
    return call(normalize_kernel, outs, (), rows_in)


def finish(params, rows_in, inverse, *parts, weight=0):
    outs = [(rows_in.shape, jnp.float32)]
    arrays = (rows_in, inverse, *parts)
    return call(finish_kernel, outs, (params,), *arrays, out_memory=None, weight=weight)[0]


def local(image_embed, text_embed, log_scale, bias):
    rows, width = image_embed.shape
    f32, bf16 = jnp.float32, jnp.bfloat16
    block = ((rows, width), f32)
    position = lax.axis_index("blk")
    column = position % ROW // 2
    odd = position % 2 == 1
    params = jnp.concatenate([jnp.exp(log_scale), bias])
    places = jnp.stack([odd, column < 2, column >= 3, column >= 1]).astype(jnp.int32)
    half = ((rows // 2, width), f32)

    y_own, y_inv = normalize(text_embed)
    y_last = moved(y_own, next_row)
    x_own, x_inv, x_0, x_1 = normalize(together(image_embed, y_own)[0], 2)
    x_cut_0 = moved(x_0, other_group)
    y_2 = moved(y_own, in_row(2))
    x_beside = moved(x_own, other_core)
    y_last, y_own, x_own, x_1, x_cut_0 = together(y_last, y_own, x_own, x_1, x_cut_0)
    for_1, for_3 = call(select_kernel, [block] * 2, (places,), y_own, y_last, weight=WEIGHT)
    y_2, x_beside, for_1, for_3, x_1 = together(y_2, x_beside, for_1, for_3, x_1)

    y_2_last = moved(y_2, next_row)
    x_cut_1 = moved(x_1, other_group)
    y_1 = moved(for_1, in_row(1))
    y_3 = moved(for_3, in_row(-1))
    x_cut_beside_0 = moved(x_cut_0, other_core)
    y_2_last, x_cut_1 = together(y_2_last, x_cut_1)
    y_2 = call(select_two_kernel, [block], (places,), y_2, y_2_last, weight=WEIGHT)[0]
    y_1, y_3, y_2, x_cut_1, x_cut_beside_0 = together(y_1, y_3, y_2, x_cut_1, x_cut_beside_0)

    x_cut_beside_1 = moved(x_cut_1, other_core)
    images = (x_own, x_cut_0, x_cut_1, x_beside, x_cut_beside_0, x_cut_beside_1)
    outs = [((4 * rows, width), bf16)] * 2 + [((3 * rows, 4 * rows), f32)] + [block] * 3
    far = call(far_kernel, outs, (params,), *images, y_1, y_3, y_2)
    x_high, x_low, g_far, gy_1, gy_3, gy_2 = together(*far)

    gy_2_last = moved(gy_2, last_row)
    back_1 = moved(gy_1, in_row(-1))
    back_3 = moved(gy_3, in_row(1))
    arrays = (y_own, y_last, y_1, y_3, y_2, x_high, x_low, g_far)
    near = call(near_kernel, [block] * 6, (params, places), *arrays)
    gx_own, gx_other, gy_here, gx_near_own, gx_near_other, gy_near = near
    gx_beside_other = moved(gx_near_other, other_core)
    gx_0, gx_1 = call(add_kernel, [half] * 2, (), gx_other, gx_beside_other)
    gx_cut_0 = moved(gx_0, other_group)
    gx_beside_own = moved(gx_near_own, other_core)
    back_1, back_3, gy_2, gy_2_last, gy_near = together(back_1, back_3, gy_2, gy_2_last, gy_near)
    gy_last = call(last_kernel, [block], (places,), gy_near, back_1, back_3, weight=WEIGHT)[0]
    for_2 = call(select_two_kernel, [block], (places,), gy_2, gy_2_last, weight=WEIGHT)[0]
    gy_last, for_2, gx_cut_0, gx_1, gx_beside_own = together(
        gy_last, for_2, gx_cut_0, gx_1, gx_beside_own
    )

    home = moved(gy_last, last_row)
    gx_cut_1 = moved(gx_1, other_group)
    back_2 = moved(for_2, in_row(2))
    gy_own = call(own_kernel, [block], (places,), gy_here, gy_near, back_1, back_3)[0]
    parts = (gx_own, gx_beside_own, gx_cut_0, gx_cut_1)
    image_grad = finish(params, x_own, x_inv, *parts, weight=WEIGHT)
    home, back_2, image_grad = together(home, back_2, image_grad)
    text_grad = finish(params, y_own, y_inv, gy_own, back_2, home)
    return (image_grad, text_grad)


def solution(mesh):
    rows = P(("cuts", "blk"), None)
    return jax.shard_map(
        local, mesh=mesh, in_specs=(rows, rows, P(), P()), out_specs=(rows, rows), check_vma=False
    )
```

```python
import jax
import jax.numpy as jnp
from jax import lax
from jax.experimental import pallas as pl
from jax.experimental.pallas import tpu as pltpu
from jax.sharding import PartitionSpec as P

GROUPS, BLOCKS, ROW = 2, 128, 8
CHUNKS = 4
W_ONE = 0
W_HOP = 300_000_000
W_LAST = 0
W_BACK = 0
W_ADD = 500_000_000
W_END = 200_000_000


def moved(block, place):
    pairs = []
    for group in range(GROUPS):
        for position in range(BLOCKS):
            to_group, to_position = place(group, position)
            pairs.append((group * BLOCKS + position, to_group * BLOCKS + to_position % BLOCKS))
    return lax.ppermute(block, ("cuts", "blk"), pairs)


def next_row(group, position):
    return (group, position + ROW) if position % 2 == 0 else (1 - group, position + ROW)


def last_row(group, position):
    return (group, position - ROW) if position % 2 == 0 else (1 - group, position - ROW)


def in_row(chips):
    return lambda group, position: (
        group,
        position // ROW * ROW + (position + 2 * chips) % ROW,
    )


def other_core(group, position):
    return group, position ^ 1


def other_group(group, position):
    return 1 - group, position


def together(*values):
    return lax.optimization_barrier(values)


def split(values):
    high = values.astype(jnp.bfloat16)
    return high, (values - high.astype(jnp.float32)).astype(jnp.bfloat16)


def dot3(a, b, b_dim):
    dims = (((1,), (b_dim,)), ((), ()))
    (a_high, a_low), (b_high, b_low) = a, b

    def one(u, v):
        return lax.dot_general(u, v, dims, preferred_element_type=jnp.float32)

    return one(a_high, b_high) + (one(a_low, b_high) + one(a_high, b_low))


def sigmoid(values):
    return 1.0 / (1.0 + jnp.exp(-values))


def normalize_kernel(in_ref, inverse_ref, *outs):
    values = in_ref[...]
    inverse = lax.rsqrt(jnp.sum(values * values, axis=-1, keepdims=True) + 1e-06)
    inverse_ref[...] = inverse
    values = values * inverse
    for at, out in enumerate(outs):
        out[...] = values[at * out.shape[0] : (at + 1) * out.shape[0], :]


def split_kernel(*refs):
    *images, high_ref, low_ref = refs
    at = 0
    for image in images:
        high, low = split(image[...])
        high_ref[at : at + image.shape[0], :] = high
        low_ref[at : at + image.shape[0], :] = low
        at += image.shape[0]


def join_kernel(first_high, first_low, *refs):
    *images, high_ref, low_ref = refs
    at = first_high.shape[0]
    high_ref[:at, :] = first_high[...]
    low_ref[:at, :] = first_low[...]
    for image in images:
        high, low = split(image[...])
        high_ref[at : at + image.shape[0], :] = high
        low_ref[at : at + image.shape[0], :] = low
        at += image.shape[0]


def far_kernel(params, *refs):
    count = (len(refs) - 3) // 2
    texts, (high_ref, low_ref, grads_ref), outs = refs[:count], refs[count:-count], refs[-count:]
    rows = texts[0].shape[0]
    image = (high_ref[...], low_ref[...])
    text = split(jnp.concatenate([ref[...] for ref in texts], axis=0))
    grads = sigmoid(params[0] * dot3(text, image, 1) + params[1])
    grads_ref[...] = grads
    to_text = dot3(split(grads), image, 0)
    for at, out in enumerate(outs):
        out[...] = to_text[at * rows : (at + 1) * rows, :]


def near_kernel(first, params, places, *refs):
    (own, last, high_ref, low_ref), outs = refs[:4], refs[4:]
    rows = own.shape[0]
    for side, grads_ref, to_text in ((0, *outs[:2]), (1, *outs[2:])):
        span = pl.ds(first + side * rows, rows)
        image = (high_ref[span, :], low_ref[span, :])
        text = own[...]
        if side == 1:
            text = jnp.where(places[0] == 1, last[...], text)
        logits = params[0] * dot3(split(text), image, 1) + params[1]
        if side == 0 and first == 0:
            row_ids = lax.broadcasted_iota(jnp.int32, logits.shape, 0)
            col_ids = lax.broadcasted_iota(jnp.int32, logits.shape, 1)
            signs = jnp.where(row_ids == col_ids, -1.0, 1.0)
            grads = signs * sigmoid(signs * logits)
        else:
            grads = sigmoid(logits)
        grads_ref[...] = grads
        to_text[...] = dot3(split(grads), image, 0)


def image_kernel(first, places, own, last, y_1, y_3, y_2, g_here, g_near, g_13, g_2, *outs):
    rows = own.shape[0]
    far = [y_1[...], y_3[...], y_2[...]]
    here = own[...]
    near = jnp.where(places[0] == 1, last[...], here)
    for side, text, mine in ((0, here, g_here), (1, near, g_near)):
        columns = pl.ds(first + side * rows, rows)
        grads = [g_13[:, columns], g_2[:, columns], mine[...]]
        grads = split(jnp.concatenate(grads, axis=0).T)
        to_image = dot3(grads, split(jnp.concatenate([*far, text], axis=0)), 0)
        mine_outs = outs[side * len(outs) // 2 : (side + 1) * len(outs) // 2]
        for at, out in enumerate(mine_outs):
            out[...] = to_image[at * out.shape[0] : (at + 1) * out.shape[0], :]


def select_kernel(places, own, last, one_ref, three_ref):
    one_ref[...] = jnp.where(places[2] == 1, last[...], own[...])
    three_ref[...] = jnp.where(places[3] == 1, last[...], own[...])


def select_two_kernel(places, two, two_last, out_ref):
    out_ref[...] = jnp.where(places[1] == 1, two_last[...], two[...])


def last_kernel(places, near_a, near_b, back_1, back_3, out_ref):
    total = jnp.where(places[0] == 1, near_a[...] + near_b[...], 0.0)
    total = total + jnp.where(places[2] == 1, back_1[...], 0.0)
    out_ref[...] = total + jnp.where(places[3] == 1, back_3[...], 0.0)


def own_kernel(places, here_a, here_b, near_a, near_b, back_1, back_3, out_ref):
    total = here_a[...] + here_b[...]
    total = total + jnp.where(places[0] == 1, 0.0, near_a[...] + near_b[...])
    total = total + jnp.where(places[2] == 1, 0.0, back_1[...])
    out_ref[...] = total + jnp.where(places[3] == 1, 0.0, back_3[...])


def add_kernel(here, beside, out_ref):
    out_ref[...] = here[...] + beside[...]


def finish_kernel(params, rows_parts, inverse_ref, *refs):
    *parts, out_ref, held, left = refs
    count = held.shape[0]
    rows = count // CHUNKS
    copies = []

    def chunk(refs, at):
        size = refs[0].shape[0]
        return refs[at * rows // size][pl.ds(at * rows % size, rows), :]

    for at in range(CHUNKS):
        span = pl.ds(at * rows, rows)
        normal = chunk(rows_parts, at)
        total = params[0] * sum(chunk(part, at) for part in parts)
        along = jnp.sum(normal * total, axis=-1, keepdims=True)
        held[span, :] = inverse_ref[span, :] * (total - normal * along)
        copies.append(
            pltpu.make_async_copy(held.at[span, :], out_ref.at[span, :], left.at[at])
        )
        copies[-1].start()
    for copy in copies:
        copy.wait()


def call(kernel, outs, scalars, *arrays, weight=0):
    vmem = pl.BlockSpec(memory_space=pltpu.VMEM)
    smem = pl.BlockSpec(memory_space=pltpu.SMEM)
    return pl.pallas_call(
        kernel,
        out_shape=[jax.ShapeDtypeStruct(shape, dtype) for shape, dtype in outs],
        in_specs=[smem] * len(scalars) + [vmem] * len(arrays),
        out_specs=[vmem] * len(outs),
        compiler_params=pltpu.CompilerParams(vmem_limit_bytes=16 * 2**20),
        cost_estimate=pl.CostEstimate(flops=weight, transcendentals=0, bytes_accessed=0),
    )(*scalars, *arrays)


def normalize(rows_in, parts):
    rows, width = rows_in.shape
    outs = [((rows, 1), jnp.float32)] + [((rows // parts, width), jnp.float32)] * parts
    return call(normalize_kernel, outs, (), rows_in)


def finish(params, rows_in, inverse, *parts, weight=0):
    groups = [part if isinstance(part, tuple) else (part,) for part in (rows_in, *parts)]
    shape = (inverse.shape[0], groups[0][0].shape[1])
    vmem = pl.BlockSpec(memory_space=pltpu.VMEM)
    arrays = [array for group in groups for array in group]

    def kernel(params_ref, inverse_ref, *refs):
        refs = list(refs)
        taken = [tuple(refs.pop(0) for _ in group) for group in groups]
        finish_kernel(params_ref, taken[0], inverse_ref, *taken[1:], *refs)

    return pl.pallas_call(
        kernel,
        out_shape=jax.ShapeDtypeStruct(shape, jnp.float32),
        in_specs=[pl.BlockSpec(memory_space=pltpu.SMEM)] + [vmem] * (1 + len(arrays)),
        out_specs=pl.BlockSpec(memory_space=pltpu.HBM),
        scratch_shapes=[pltpu.VMEM(shape, jnp.float32), pltpu.SemaphoreType.DMA((CHUNKS,))],
        compiler_params=pltpu.CompilerParams(vmem_limit_bytes=16 * 2**20),
        cost_estimate=pl.CostEstimate(flops=weight, transcendentals=0, bytes_accessed=0),
    )(params, inverse, *arrays)


def local(image_embed, text_embed, log_scale, bias):
    rows, width = image_embed.shape
    f32, bf16 = jnp.float32, jnp.bfloat16
    block = ((rows, width), f32)
    position = lax.axis_index("blk")
    column = position % ROW // 2
    odd = position % 2 == 1
    params = jnp.concatenate([jnp.exp(log_scale), bias])
    places = jnp.stack([odd, column < 2, column >= 3, column >= 1]).astype(jnp.int32)
    half = ((rows // 2, width), f32)

    square = ((rows, rows), f32)
    pair = ((2 * rows, width), bf16)

    y_inv, y_own = normalize(text_embed, 1)
    y_last = moved(y_own, next_row)
    y_2 = moved(y_own, in_row(2))
    x_inv, x_0, x_1 = normalize(together(image_embed, y_own)[0], 2)
    x_cut_0 = moved(x_0, other_group)
    x_beside_0 = moved(x_0, other_core)
    x_beside_1 = moved(x_1, other_core)
    y_2_last = moved(y_2, next_row)
    y_last, y_own, y_2, x_0, x_1, x_beside_0, x_beside_1, x_cut_0 = together(
        y_last, y_own, y_2, x_0, x_1, x_beside_0, x_beside_1, x_cut_0
    )
    for_1, for_3 = call(select_kernel, [block] * 2, (places,), y_own, y_last, weight=W_ONE)
    y_1 = moved(for_1, in_row(1))
    y_3 = moved(for_3, in_row(-1))
    x_cut_0, x_1, y_own, _ = together(x_cut_0, x_1, y_own, for_1)
    x_cut_1 = moved(x_1, other_group)
    x_cut_beside_0 = moved(x_cut_0, other_core)
    xa_high, xa_low = call(split_kernel, [pair] * 2, (), x_0, x_1, x_beside_0, x_beside_1)
    arrays = (y_own, y_last, xa_high, xa_low)
    kernel = lambda *refs: near_kernel(0, *refs)
    near = call(kernel, [square, block] * 2, (params, places), *arrays)
    ga_here, gya_here, ga_near, gya_near = near
    y_2 = call(select_two_kernel, [block], (places,), y_2, y_2_last, weight=W_HOP)[0]
    y_1, y_3, y_2, x_cut_1, x_cut_beside_0, ga_here = together(
        y_1, y_3, y_2, x_cut_1, x_cut_beside_0, ga_here
    )

    x_cut_beside_1 = moved(x_cut_1, other_core)
    images = (x_cut_0, x_cut_1, x_cut_beside_0, x_cut_beside_1)
    outs = [((4 * rows, width), bf16)] * 2
    x_high, x_low = call(join_kernel, outs, (), xa_high, xa_low, *images)
    outs = [((rows, 4 * rows), f32), block]
    g_2, gy_2 = call(far_kernel, outs, (params,), y_2, x_high, x_low)
    gy_2_last = moved(gy_2, last_row)
    g_2, y_1, y_3 = together(g_2, y_1, y_3)
    outs = [((2 * rows, 4 * rows), f32)] + [block] * 2
    g_13, gy_1, gy_3 = call(far_kernel, outs, (params,), y_1, y_3, x_high, x_low)
    back_1 = moved(gy_1, in_row(-1))
    back_3 = moved(gy_3, in_row(1))

    g_13, x_high = together(g_13, x_high)
    arrays = (y_own, y_last, x_high, x_low)
    kernel = lambda *refs: near_kernel(2 * rows, *refs)
    near = call(kernel, [square, block] * 2, (params, places), *arrays)
    gb_here, gyb_here, gb_near, gyb_near = near
    arrays = (y_own, y_last, y_1, y_3, y_2, gb_here, gb_near, g_13, g_2)
    kernel = lambda *refs: image_kernel(2 * rows, *refs)
    gx_0, gx_1, gx_near_0, gx_near_1 = call(kernel, [half] * 4, (places,), *arrays)
    gx_beside_0 = moved(gx_near_0, other_core)
    gx_beside_1 = moved(gx_near_1, other_core)
    gx_0 = call(add_kernel, [half], (), gx_0, gx_beside_0)[0]
    gx_cut_0 = moved(gx_0, other_group)
    gx_1, y_1, y_3 = together(gx_1, y_1, y_3)
    arrays = (y_own, y_last, y_1, y_3, y_2, ga_here, ga_near, g_13, g_2)
    kernel = lambda *refs: image_kernel(0, *refs)
    gx_own, gx_near_own = call(kernel, [block] * 2, (places,), *arrays)
    gx_near_own, gx_1 = together(gx_near_own, gx_1)

    gy_2, gy_2_last = together(gy_2, gy_2_last)
    for_2 = call(select_two_kernel, [block], (places,), gy_2, gy_2_last, weight=W_BACK)[0]
    back_1, back_3, for_2, gx_near_own, gx_1, gx_beside_1 = together(
        back_1, back_3, for_2, gx_near_own, gx_1, gx_beside_1
    )
    arrays = (gya_near, gyb_near, back_1, back_3)
    gy_last = call(last_kernel, [block], (places,), *arrays, weight=W_LAST)[0]
    arrays = (gya_here, gyb_here, *arrays)
    gy_own = call(own_kernel, [block], (places,), *arrays)[0]
    home = moved(gy_last, last_row)
    back_2 = moved(for_2, in_row(2))
    gx_beside_own = moved(gx_near_own, other_core)
    gx_cut_0, gx_1 = together(gx_cut_0, gx_1)
    gx_1 = call(add_kernel, [half], (), gx_1, gx_beside_1, weight=W_ADD)[0]
    gx_cut_1 = moved(gx_1, other_group)
    home, gx_cut_1, gy_own = together(home, gx_cut_1, gy_own)
    parts = (gx_own, gx_beside_own, (gx_cut_0, gx_cut_1))
    image_grad = finish(params, (x_0, x_1), x_inv, *parts, weight=W_END)
    back_2, image_grad, gy_own = together(back_2, image_grad, gy_own)
    text_grad = finish(params, y_own, y_inv, gy_own, back_2, home)
    return (image_grad, text_grad)


def solution(mesh):
    rows = P(("cuts", "blk"), None)
    return jax.shard_map(
        local, mesh=mesh, in_specs=(rows, rows, P(), P()), out_specs=(rows, rows), check_vma=False
    )
```

```python
import jax
import jax.numpy as jnp
from jax import lax
from jax.experimental import pallas as pl
from jax.experimental.pallas import tpu as pltpu
from jax.sharding import PartitionSpec as P

GROUPS, BLOCKS, ROW = 2, 128, 8
W_ONE = 0
W_HOP = 300_000_000
W_CUT = 600_000_000
W_LAST = 0
W_BACK = 0
W_HALF = 1_000_000_000
W_END = 1_000_000_000
W_HOME = 100_000_000


def moved(block, place):
    pairs = []
    for group in range(GROUPS):
        for position in range(BLOCKS):
            to_group, to_position = place(group, position)
            pairs.append((group * BLOCKS + position, to_group * BLOCKS + to_position % BLOCKS))
    return lax.ppermute(block, ("cuts", "blk"), pairs)


def next_row(group, position):
    return (group, position + ROW) if position % 2 == 0 else (1 - group, position + ROW)


def last_row(group, position):
    return (group, position - ROW) if position % 2 == 0 else (1 - group, position - ROW)


def in_row(chips):
    return lambda group, position: (
        group,
        position // ROW * ROW + (position + 2 * chips) % ROW,
    )


def other_core(group, position):
    return group, position ^ 1


def other_group(group, position):
    return 1 - group, position


def together(*values):
    return lax.optimization_barrier(values)


def split(values):
    high = values.astype(jnp.bfloat16)
    return high, (values - high.astype(jnp.float32)).astype(jnp.bfloat16)


def dot3(a, b, b_dim):
    dims = (((1,), (b_dim,)), ((), ()))
    (a_high, a_low), (b_high, b_low) = a, b

    def one(u, v):
        return lax.dot_general(u, v, dims, preferred_element_type=jnp.float32)

    return one(a_high, b_high) + (one(a_low, b_high) + one(a_high, b_low))


def places():
    position = lax.axis_index("blk")
    column = position % ROW // 2
    return position % 2 == 1, column < 2, column >= 3, column >= 1


def sigmoid(values):
    return 1.0 / (1.0 + jnp.exp(-values))


def params_kernel(log_scale, bias, out_ref):
    row_ids = lax.broadcasted_iota(jnp.int32, out_ref.shape, 0)
    scale = jnp.exp(jnp.zeros(out_ref.shape, jnp.float32) + log_scale[0])
    out_ref[...] = jnp.where(row_ids == 0, scale, bias[0])


def normalize_kernel(_, in_ref, inverse_ref, *outs):
    values = in_ref[...]
    inverse = lax.rsqrt(jnp.sum(values * values, axis=-1, keepdims=True) + 1e-06)
    inverse_ref[...] = inverse
    values = values * inverse
    for at, out in enumerate(outs):
        out[...] = values[at * out.shape[0] : (at + 1) * out.shape[0], :]


def split_kernel(*refs):
    *images, high_ref, low_ref = refs
    at = 0
    for image in images:
        high, low = split(image[...])
        high_ref[at : at + image.shape[0], :] = high
        low_ref[at : at + image.shape[0], :] = low
        at += image.shape[0]


def join_kernel(first_high, first_low, second_high, second_low, *refs):
    *images, high_ref, low_ref = refs
    middle = first_high.shape[0]
    at = middle + second_high.shape[0]
    high_ref[:middle, :] = first_high[...]
    low_ref[:middle, :] = first_low[...]
    high_ref[middle:at, :] = second_high[...]
    low_ref[middle:at, :] = second_low[...]
    for image in images:
        high, low = split(image[...])
        high_ref[at : at + image.shape[0], :] = high
        low_ref[at : at + image.shape[0], :] = low
        at += image.shape[0]


def far_kernel(params, *refs):
    count = (len(refs) - 3) // 2
    texts, (high_ref, low_ref, grads_ref), outs = refs[:count], refs[count:-count], refs[-count:]
    rows = texts[0].shape[0]
    image = (high_ref[...], low_ref[...])
    text = split(jnp.concatenate([ref[...] for ref in texts], axis=0))
    grads = sigmoid(params[0:1, 0:1] * dot3(text, image, 1) + params[1:2, 0:1])
    grads_ref[...] = grads
    to_text = dot3(split(grads), image, 0)
    for at, out in enumerate(outs):
        out[...] = to_text[at * rows : (at + 1) * rows, :]


def near_kernel(first, params, *refs):
    (own, last, high_ref, low_ref), outs = refs[:4], refs[4:]
    rows = own.shape[0]
    for side, grads_ref, to_text in ((0, *outs[:2]), (1, *outs[2:])):
        span = pl.ds(first + side * rows, rows)
        image = (high_ref[span, :], low_ref[span, :])
        text = own[...]
        if side == 1:
            text = jnp.where(places()[0], last[...], text)
        logits = params[0:1, 0:1] * dot3(split(text), image, 1) + params[1:2, 0:1]
        if side == 0 and first == 0:
            row_ids = lax.broadcasted_iota(jnp.int32, logits.shape, 0)
            col_ids = lax.broadcasted_iota(jnp.int32, logits.shape, 1)
            signs = jnp.where(row_ids == col_ids, -1.0, 1.0)
            grads = signs * sigmoid(signs * logits)
        else:
            grads = sigmoid(logits)
        grads_ref[...] = grads
        to_text[...] = dot3(split(grads), image, 0)


def image_kernel(first, own, last, y_1, y_3, y_2, g_here, g_near, g_13, g_2, *outs):
    rows = own.shape[0]
    far = [y_1[...], y_3[...], y_2[...]]
    here = own[...]
    near = jnp.where(places()[0], last[...], here)
    for side, text, mine in ((0, here, g_here), (1, near, g_near)):
        columns = pl.ds(first + side * rows, rows)
        grads = [g_13[:, columns], g_2[:, columns], mine[...]]
        grads = split(jnp.concatenate(grads, axis=0).T)
        to_image = dot3(grads, split(jnp.concatenate([*far, text], axis=0)), 0)
        mine_outs = outs[side * len(outs) // 2 : (side + 1) * len(outs) // 2]
        for at, out in enumerate(mine_outs):
            out[...] = to_image[at * out.shape[0] : (at + 1) * out.shape[0], :]


def select_kernel(own, last, one_ref, three_ref):
    one_ref[...] = jnp.where(places()[2], last[...], own[...])
    three_ref[...] = jnp.where(places()[3], last[...], own[...])


def select_two_kernel(two, two_last, out_ref):
    out_ref[...] = jnp.where(places()[1], two_last[...], two[...])


def last_kernel(near_a, near_b, back_1, back_3, out_ref):
    total = jnp.where(places()[0], near_a[...] + near_b[...], 0.0)
    total = total + jnp.where(places()[2], back_1[...], 0.0)
    out_ref[...] = total + jnp.where(places()[3], back_3[...], 0.0)


def own_kernel(here_a, here_b, near_a, near_b, back_1, back_3, out_ref):
    total = here_a[...] + here_b[...]
    total = total + jnp.where(places()[0], 0.0, near_a[...] + near_b[...])
    total = total + jnp.where(places()[2], 0.0, back_1[...])
    out_ref[...] = total + jnp.where(places()[3], 0.0, back_3[...])


def add_three_kernel(one, two, three, out_ref):
    out_ref[...] = one[...] + two[...] + three[...]


def add_kernel(here, beside, out_ref):
    out_ref[...] = here[...] + beside[...]


def finish_kernel(params, y, y_inv, *refs):
    y_parts, x_halves, x_inv, x_totals, outs, (held, left) = (
        refs[:2],
        refs[2:4],
        refs[4],
        refs[5:7],
        refs[7:9],
        refs[9:],
    )
    rows = x_halves[0].shape[0]
    copies = []
    for at in range(4):
        side, first = at // 2, at % 2 * rows
        span = pl.ds(first, rows)
        if side == 0:
            normal, inverse = x_halves[at][...], x_inv[span, :]
            total = x_totals[at][...]
        else:
            normal, inverse = y[span, :], y_inv[span, :]
            total = y_parts[0][span, :] + y_parts[1][span, :]
        total = params[0:1, 0:1] * total
        along = jnp.sum(normal * total, axis=-1, keepdims=True)
        held[side, span, :] = inverse * (total - normal * along)
        copies.append(
            pltpu.make_async_copy(
                held.at[side, span, :], outs[side].at[span, :], left.at[at]
            )
        )
        copies[-1].start()
    for copy in copies:
        copy.wait()


def call(kernel, outs, *arrays, scalars=(), weight=0):
    vmem = pl.BlockSpec(memory_space=pltpu.VMEM)
    smem = pl.BlockSpec(memory_space=pltpu.SMEM)
    return pl.pallas_call(
        kernel,
        out_shape=[jax.ShapeDtypeStruct(shape, dtype) for shape, dtype in outs],
        in_specs=[smem] * len(scalars) + [vmem] * len(arrays),
        out_specs=[vmem] * len(outs),
        compiler_params=pltpu.CompilerParams(vmem_limit_bytes=16 * 2**20),
        cost_estimate=pl.CostEstimate(flops=weight, transcendentals=0, bytes_accessed=0),
    )(*scalars, *arrays)


def finish(*arrays):
    shape = arrays[1].shape
    hbm = pl.BlockSpec(memory_space=pltpu.HBM)
    return pl.pallas_call(
        finish_kernel,
        out_shape=[jax.ShapeDtypeStruct(shape, jnp.float32)] * 2,
        in_specs=[pl.BlockSpec(memory_space=pltpu.VMEM)] * len(arrays),
        out_specs=[hbm] * 2,
        scratch_shapes=[pltpu.VMEM((2, *shape), jnp.float32), pltpu.SemaphoreType.DMA((4,))],
        compiler_params=pltpu.CompilerParams(vmem_limit_bytes=16 * 2**20),
        cost_estimate=pl.CostEstimate(flops=0, transcendentals=0, bytes_accessed=0),
    )(*arrays)


def local(image_embed, text_embed, log_scale, bias):
    rows, width = image_embed.shape
    f32, bf16 = jnp.float32, jnp.bfloat16
    block = ((rows, width), f32)
    half = ((rows // 2, width), f32)

    square = ((rows, rows), f32)
    pair = ((2 * rows, width), bf16)

    outs = [((rows, 1), f32), block]
    y_inv, y_own = call(lambda *refs: normalize_kernel(None, *refs), outs, text_embed)
    outs = [((rows, 1), f32), half, half]
    x_inv, x_0, x_1 = call(normalize_kernel, outs, y_inv, image_embed)
    params = call(params_kernel, [((8, 128), f32)], scalars=(log_scale, bias))
    y_last = moved(y_own, next_row)
    y_2 = moved(y_own, in_row(2))
    x_cut_0 = moved(x_0, other_group)
    x_beside_0 = moved(x_0, other_core)
    x_beside_1 = moved(x_1, other_core)
    y_2_last = moved(y_2, next_row)
    y_last, y_own, y_2, x_0, x_1, x_beside_0, x_beside_1 = together(
        y_last, y_own, y_2, x_0, x_1, x_beside_0, x_beside_1
    )
    for_1, for_3 = call(select_kernel, [block] * 2, y_own, y_last, weight=W_ONE)
    y_1 = moved(for_1, in_row(1))
    y_3 = moved(for_3, in_row(-1))
    x_cut_0, x_1, y_own, _ = together(x_cut_0, x_1, y_own, for_1)
    xc_high, xc_low = call(
        split_kernel, [((rows // 2, width), bf16)] * 2, x_cut_0, weight=W_CUT
    )
    x_1, xc_high, x_cut_0 = together(x_1, xc_high, x_cut_0)
    x_cut_1 = moved(x_1, other_group)
    x_cut_beside_0 = moved(x_cut_0, other_core)
    xa_high, xa_low = call(split_kernel, [pair] * 2, x_0, x_1, x_beside_0, x_beside_1)
    arrays = (y_own, y_last, xa_high, xa_low)
    kernel = lambda *refs: near_kernel(0, *refs)
    near = call(kernel, [square, block] * 2, *params, *arrays)
    ga_here, gya_here, ga_near, gya_near = near
    y_2 = call(select_two_kernel, [block], y_2, y_2_last, weight=W_HOP)[0]
    y_1, y_3, y_2, x_cut_1, x_cut_beside_0, ga_here = together(
        y_1, y_3, y_2, x_cut_1, x_cut_beside_0, ga_here
    )

    x_cut_beside_1 = moved(x_cut_1, other_core)
    images = (x_cut_1, x_cut_beside_0, x_cut_beside_1)
    outs = [((4 * rows, width), bf16)] * 2
    x_high, x_low = call(join_kernel, outs, xa_high, xa_low, xc_high, xc_low, *images)
    outs = [((2 * rows, 4 * rows), f32)] + [block] * 2
    g_13, gy_1, gy_3 = call(far_kernel, outs, *params, y_1, y_3, x_high, x_low)
    back_1 = moved(gy_1, in_row(-1))
    back_3 = moved(gy_3, in_row(1))
    g_13, y_2 = together(g_13, y_2)
    outs = [((rows, 4 * rows), f32), block]
    g_2, gy_2 = call(far_kernel, outs, *params, y_2, x_high, x_low)
    gy_2_last = moved(gy_2, last_row)

    g_2, x_high = together(g_2, x_high)
    arrays = (y_own, y_last, x_high, x_low)
    kernel = lambda *refs: near_kernel(2 * rows, *refs)
    near = call(kernel, [square, block] * 2, *params, *arrays)
    gb_here, gyb_here, gb_near, gyb_near = near
    arrays = (y_own, y_last, y_1, y_3, y_2, gb_here, gb_near, g_13, g_2)
    kernel = lambda *refs: image_kernel(2 * rows, *refs)
    gx_0, gx_1, gx_near_0, gx_near_1 = call(kernel, [half] * 4, *arrays)
    gx_beside_0 = moved(gx_near_0, other_core)
    gx_beside_1 = moved(gx_near_1, other_core)
    gx_0 = call(add_kernel, [half], gx_0, gx_beside_0)[0]
    gx_cut_0 = moved(gx_0, other_group)
    gx_1, y_1, y_3 = together(gx_1, y_1, y_3)
    arrays = (y_own, y_last, y_1, y_3, y_2, ga_here, ga_near, g_13, g_2)
    kernel = lambda *refs: image_kernel(0, *refs)
    outs = call(kernel, [half] * 4, *arrays)
    gx_own_0, gx_own_1, gx_near_own_0, gx_near_own_1 = outs
    gx_1 = call(add_kernel, [half], gx_1, gx_beside_1)[0]
    back_1, back_3, gx_near_own_0, gx_near_own_1, gx_1 = together(
        back_1, back_3, gx_near_own_0, gx_near_own_1, gx_1
    )
    arrays = (gya_near, gyb_near, back_1, back_3)
    gy_last = call(last_kernel, [block], *arrays, weight=W_LAST)[0]
    home = moved(gy_last, last_row)
    gy_2, gy_2_last, gx_1, gx_near_own_0, gx_near_own_1, _ = together(
        gy_2, gy_2_last, gx_1, gx_near_own_0, gx_near_own_1, gy_last
    )
    for_2 = call(select_two_kernel, [block], gy_2, gy_2_last, weight=W_BACK)[0]
    back_2 = moved(for_2, in_row(2))
    gx_cut_1 = moved(gx_1, other_group)
    gx_beside_own_0 = moved(gx_near_own_0, other_core)
    gx_beside_own_1 = moved(gx_near_own_1, other_core)
    arrays = (gya_here, gyb_here, *arrays)
    gy_own = call(own_kernel, [block], *arrays)[0]
    gx_cut_0, gy_own = together(gx_cut_0, gy_own)
    parts = (gx_own_0, gx_beside_own_0, gx_cut_0)
    image_0 = call(add_three_kernel, [half], *parts, weight=W_HALF)[0]
    gx_cut_1, image_0 = together(gx_cut_1, image_0)
    parts = (gx_own_1, gx_beside_own_1, gx_cut_1)
    image_1 = call(add_three_kernel, [half], *parts, weight=W_END)[0]
    home, gy_own, image_0, image_1 = together(home, gy_own, image_0, image_1)
    gy_own = call(add_kernel, [block], gy_own, home, weight=W_HOME)[0]
    back_2, gy_own, image_0, image_1 = together(back_2, gy_own, image_0, image_1)
    return tuple(
        finish(*params, y_own, y_inv, gy_own, back_2, x_0, x_1, x_inv, image_0, image_1)
    )


def solution(mesh):
    rows = P(("cuts", "blk"), None)
    return jax.shard_map(
        local, mesh=mesh, in_specs=(rows, rows, P(), P()), out_specs=(rows, rows), check_vma=False
    )
```

```python
import jax
import jax.numpy as jnp
from jax import lax
from jax.experimental import pallas as pl
from jax.experimental.pallas import tpu as pltpu
from jax.sharding import PartitionSpec as P

GROUPS, BLOCKS, ROW = 2, 128, 8
FIRST = 64
W_ONE = 0
W_HOP = 0
W_CUT = 300_000_000
W_FAR = 3000_000_000
W_LAST = 0
W_BACK = 0
W_HALF = 1_000_000_000
W_END = 1_000_000_000
W_HOME = 100_000_000


def moved(block, place):
    pairs = []
    for group in range(GROUPS):
        for position in range(BLOCKS):
            to_group, to_position = place(group, position)
            pairs.append((group * BLOCKS + position, to_group * BLOCKS + to_position % BLOCKS))
    return lax.ppermute(block, ("cuts", "blk"), pairs)


def next_row(group, position):
    return (group, position + ROW) if position % 2 == 0 else (1 - group, position + ROW)


def last_row(group, position):
    return (group, position - ROW) if position % 2 == 0 else (1 - group, position - ROW)


def in_row(chips):
    return lambda group, position: (
        group,
        position // ROW * ROW + (position + 2 * chips) % ROW,
    )


def other_core(group, position):
    return group, position ^ 1


def other_group(group, position):
    return 1 - group, position


def together(*values):
    return lax.optimization_barrier(values)


def split(values):
    high = values.astype(jnp.bfloat16)
    return high, (values - high.astype(jnp.float32)).astype(jnp.bfloat16)


def dot3(a, b, b_dim):
    dims = (((1,), (b_dim,)), ((), ()))
    (a_high, a_low), (b_high, b_low) = a, b

    def one(u, v):
        return lax.dot_general(u, v, dims, preferred_element_type=jnp.float32)

    return one(a_high, b_high) + (one(a_low, b_high) + one(a_high, b_low))


def places():
    position = lax.axis_index("blk")
    column = position % ROW // 2
    return position % 2 == 1, column < 2, column >= 3, column >= 1


def sigmoid(values):
    return 1.0 / (1.0 + jnp.exp(-values))


def params_kernel(log_scale, bias, out_ref):
    row_ids = lax.broadcasted_iota(jnp.int32, out_ref.shape, 0)
    scale = jnp.exp(jnp.zeros(out_ref.shape, jnp.float32) + log_scale[0])
    out_ref[...] = jnp.where(row_ids == 0, scale, bias[0])


def image_norm_kernel(_, in_ref, inverse_ref, *outs):
    normalize_kernel(in_ref, inverse_ref, *outs)


def normalize_kernel(in_ref, inverse_ref, *outs):
    values = in_ref[...]
    inverse = lax.rsqrt(jnp.sum(values * values, axis=-1, keepdims=True) + 1e-06)
    inverse_ref[...] = inverse
    values = values * inverse
    at = 0
    for out in outs:
        out[...] = values[at : at + out.shape[0], :]
        at = (at + out.shape[0]) % values.shape[0]


def split_kernel(*refs):
    *images, high_ref, low_ref = refs
    at = 0
    for image in images:
        high, low = split(image[...])
        high_ref[at : at + image.shape[0], :] = high
        low_ref[at : at + image.shape[0], :] = low
        at += image.shape[0]


def join_kernel(first_high, first_low, second_high, second_low, *refs):
    *images, high_ref, low_ref = refs
    middle = first_high.shape[0]
    at = middle + second_high.shape[0]
    high_ref[:middle, :] = first_high[...]
    low_ref[:middle, :] = first_low[...]
    high_ref[middle:at, :] = second_high[...]
    low_ref[middle:at, :] = second_low[...]
    for image in images:
        high, low = split(image[...])
        high_ref[at : at + image.shape[0], :] = high
        low_ref[at : at + image.shape[0], :] = low
        at += image.shape[0]


def far_kernel(params, *refs):
    count = (len(refs) - 3) // 2
    texts, (high_ref, low_ref, grads_ref), outs = refs[:count], refs[count:-count], refs[-count:]
    rows = texts[0].shape[0]
    image = (high_ref[...], low_ref[...])
    text = split(jnp.concatenate([ref[...] for ref in texts], axis=0))
    grads = sigmoid(params[0:1, 0:1] * dot3(text, image, 1) + params[1:2, 0:1])
    grads_ref[...] = grads
    to_text = dot3(split(grads), image, 0)
    for at, out in enumerate(outs):
        out[...] = to_text[at * rows : (at + 1) * rows, :]


def near_kernel(first, params, *refs):
    (own, last, high_ref, low_ref), outs = refs[:4], refs[4:]
    rows = own.shape[0]
    for side, grads_ref, to_text in ((0, *outs[:2]), (1, *outs[2:])):
        span = pl.ds(first + side * rows, rows)
        image = (high_ref[span, :], low_ref[span, :])
        text = own[...]
        if side == 1:
            text = jnp.where(places()[0], last[...], text)
        logits = params[0:1, 0:1] * dot3(split(text), image, 1) + params[1:2, 0:1]
        if side == 0 and first == 0:
            row_ids = lax.broadcasted_iota(jnp.int32, logits.shape, 0)
            col_ids = lax.broadcasted_iota(jnp.int32, logits.shape, 1)
            signs = jnp.where(row_ids == col_ids, -1.0, 1.0)
            grads = signs * sigmoid(signs * logits)
        else:
            grads = sigmoid(logits)
        grads_ref[...] = grads
        to_text[...] = dot3(split(grads), image, 0)


def image_kernel(first, own, last, y_1, y_3, y_2, g_here, g_near, g_13, g_2, *outs):
    rows = own.shape[0]
    far = [y_1[...], y_3[...], y_2[...]]
    here = own[...]
    near = jnp.where(places()[0], last[...], here)
    for side, text, mine in ((0, here, g_here), (1, near, g_near)):
        columns = pl.ds(first + side * rows, rows)
        grads = [g_13[:, columns], g_2[:, columns], mine[...]]
        grads = split(jnp.concatenate(grads, axis=0).T)
        to_image = dot3(grads, split(jnp.concatenate([*far, text], axis=0)), 0)
        at = 0
        for out in outs[side * len(outs) // 2 : (side + 1) * len(outs) // 2]:
            out[...] = to_image[at : at + out.shape[0], :]
            at += out.shape[0]


def select_kernel(own, last, one_ref, three_ref):
    one_ref[...] = jnp.where(places()[2], last[...], own[...])
    three_ref[...] = jnp.where(places()[3], last[...], own[...])


def select_two_kernel(two, two_last, out_ref):
    out_ref[...] = jnp.where(places()[1], two_last[...], two[...])


def last_kernel(near_a, near_b, back_1, back_3, out_ref):
    total = jnp.where(places()[0], near_a[...] + near_b[...], 0.0)
    total = total + jnp.where(places()[2], back_1[...], 0.0)
    out_ref[...] = total + jnp.where(places()[3], back_3[...], 0.0)


def own_kernel(here_a, here_b, near_a, near_b, back_1, back_3, out_ref):
    total = here_a[...] + here_b[...]
    total = total + jnp.where(places()[0], 0.0, near_a[...] + near_b[...])
    total = total + jnp.where(places()[2], 0.0, back_1[...])
    out_ref[...] = total + jnp.where(places()[3], 0.0, back_3[...])


def add_three_kernel(one, two, three, out_ref):
    out_ref[...] = one[...] + two[...] + three[...]


def add_kernel(here, beside, out_ref):
    out_ref[...] = here[...] + beside[...]


def finish_kernel(params, y, y_inv, *refs):
    y_parts, x_halves, x_inv, x_totals, outs, (held, left) = (
        refs[:2],
        refs[2:4],
        refs[4],
        refs[5:7],
        refs[7:9],
        refs[9:],
    )
    copies = []
    spans = [(0, at * y.shape[0] // 2, y.shape[0] // 2) for at in (0, 1)]
    spans += [(1, 0, x_halves[0].shape[0]), (1, x_halves[0].shape[0], x_halves[1].shape[0])]
    for at, (side, first, rows) in enumerate(spans):
        span = pl.ds(first, rows)
        if side == 1:
            normal, inverse = x_halves[at - 2][...], x_inv[span, :]
            total = x_totals[at - 2][...]
        else:
            normal, inverse = y[span, :], y_inv[span, :]
            total = y_parts[0][span, :] + y_parts[1][span, :]
        total = params[0:1, 0:1] * total
        along = jnp.sum(normal * total, axis=-1, keepdims=True)
        held[side, span, :] = inverse * (total - normal * along)
        copies.append(
            pltpu.make_async_copy(
                held.at[side, span, :], outs[1 - side].at[span, :], left.at[at]
            )
        )
        copies[-1].start()
    for copy in copies:
        copy.wait()


def call(kernel, outs, *arrays, scalars=(), weight=0):
    vmem = pl.BlockSpec(memory_space=pltpu.VMEM)
    smem = pl.BlockSpec(memory_space=pltpu.SMEM)
    return pl.pallas_call(
        kernel,
        out_shape=[jax.ShapeDtypeStruct(shape, dtype) for shape, dtype in outs],
        in_specs=[smem] * len(scalars) + [vmem] * len(arrays),
        out_specs=[vmem] * len(outs),
        compiler_params=pltpu.CompilerParams(vmem_limit_bytes=16 * 2**20),
        cost_estimate=pl.CostEstimate(flops=weight, transcendentals=0, bytes_accessed=0),
    )(*scalars, *arrays)


def finish(*arrays):
    shape = arrays[1].shape
    hbm = pl.BlockSpec(memory_space=pltpu.HBM)
    return pl.pallas_call(
        finish_kernel,
        out_shape=[jax.ShapeDtypeStruct(shape, jnp.float32)] * 2,
        in_specs=[pl.BlockSpec(memory_space=pltpu.VMEM)] * len(arrays),
        out_specs=[hbm] * 2,
        scratch_shapes=[pltpu.VMEM((2, *shape), jnp.float32), pltpu.SemaphoreType.DMA((4,))],
        compiler_params=pltpu.CompilerParams(vmem_limit_bytes=16 * 2**20),
        cost_estimate=pl.CostEstimate(flops=0, transcendentals=0, bytes_accessed=0),
    )(*arrays)


def local(image_embed, text_embed, log_scale, bias):
    rows, width = image_embed.shape
    f32, bf16 = jnp.float32, jnp.bfloat16
    block = ((rows, width), f32)

    square = ((rows, rows), f32)
    pair = ((2 * rows, width), bf16)

    outs = [((rows, 1), f32), block]
    y_inv, y_own = call(normalize_kernel, outs, text_embed)
    first, second = ((FIRST, width), f32), ((rows - FIRST, width), f32)
    outs = [((rows, 1), f32), first, second]
    x_inv, x_0, x_1 = call(image_norm_kernel, outs, y_inv, image_embed)
    params = call(params_kernel, [((8, 128), f32)], scalars=(log_scale, bias))
    y_last = moved(y_own, next_row)
    y_2 = moved(y_own, in_row(2))
    x_cut_0 = moved(x_0, other_group)
    x_beside_0 = moved(x_0, other_core)
    x_beside_1 = moved(x_1, other_core)
    y_2_last = moved(y_2, next_row)
    y_last, y_own, x_0, x_1, x_beside_0, x_beside_1 = together(
        y_last, y_own, x_0, x_1, x_beside_0, x_beside_1
    )
    for_1, for_3 = call(select_kernel, [block] * 2, y_own, y_last, weight=W_ONE)
    y_1 = moved(for_1, in_row(1))
    y_3 = moved(for_3, in_row(-1))
    x_cut_0, x_1, y_own, _ = together(x_cut_0, x_1, y_own, for_1)
    xc_high, xc_low = call(
        split_kernel, [((FIRST, width), bf16)] * 2, x_cut_0, weight=W_CUT
    )
    x_1, xc_high, x_cut_0 = together(x_1, xc_high, x_cut_0)
    x_cut_1 = moved(x_1, other_group)
    x_cut_beside_0 = moved(x_cut_0, other_core)
    xa_high, xa_low = call(split_kernel, [pair] * 2, x_0, x_1, x_beside_0, x_beside_1)
    arrays = (y_own, y_last, xa_high, xa_low)
    kernel = lambda *refs: near_kernel(0, *refs)
    near = call(kernel, [square, block] * 2, *params, *arrays)
    ga_here, gya_here, ga_near, gya_near = near
    y_1, y_3, x_cut_1, x_cut_beside_0, ga_here = together(
        y_1, y_3, x_cut_1, x_cut_beside_0, ga_here
    )

    x_cut_beside_1 = moved(x_cut_1, other_core)
    images = (x_cut_1, x_cut_beside_0, x_cut_beside_1)
    outs = [((4 * rows, width), bf16)] * 2
    x_high, x_low = call(join_kernel, outs, xa_high, xa_low, xc_high, xc_low, *images)
    outs = [((2 * rows, 4 * rows), f32)] + [block] * 2
    arrays = (*params, y_1, y_3, x_high, x_low)
    g_13, gy_1, gy_3 = call(far_kernel, outs, *arrays, weight=W_FAR)
    back_1 = moved(gy_1, in_row(-1))
    back_3 = moved(gy_3, in_row(1))
    g_13, y_2, y_2_last = together(g_13, y_2, y_2_last)
    y_2 = call(select_two_kernel, [block], y_2, y_2_last, weight=W_HOP)[0]
    outs = [((rows, 4 * rows), f32), block]
    g_2, gy_2 = call(far_kernel, outs, *params, y_2, x_high, x_low)
    gy_2_last = moved(gy_2, last_row)

    g_2, x_high = together(g_2, x_high)
    arrays = (y_own, y_last, x_high, x_low)
    kernel = lambda *refs: near_kernel(2 * rows, *refs)
    near = call(kernel, [square, block] * 2, *params, *arrays)
    gb_here, gyb_here, gb_near, gyb_near = near
    arrays = (y_own, y_last, y_1, y_3, y_2, gb_here, gb_near, g_13, g_2)
    kernel = lambda *refs: image_kernel(2 * rows, *refs)
    gx_0, gx_1, gx_near_0, gx_near_1 = call(kernel, [first, second] * 2, *arrays)
    gx_beside_0 = moved(gx_near_0, other_core)
    gx_beside_1 = moved(gx_near_1, other_core)
    gx_0 = call(add_kernel, [first], gx_0, gx_beside_0)[0]
    gx_cut_0 = moved(gx_0, other_group)
    gx_1, y_1, y_3 = together(gx_1, y_1, y_3)
    arrays = (y_own, y_last, y_1, y_3, y_2, ga_here, ga_near, g_13, g_2)
    kernel = lambda *refs: image_kernel(0, *refs)
    outs = call(kernel, [first, second] * 2, *arrays)
    gx_own_0, gx_own_1, gx_near_own_0, gx_near_own_1 = outs
    gx_1 = call(add_kernel, [second], gx_1, gx_beside_1)[0]
    back_1, back_3, gx_near_own_0, gx_near_own_1, gx_1 = together(
        back_1, back_3, gx_near_own_0, gx_near_own_1, gx_1
    )
    arrays = (gya_near, gyb_near, back_1, back_3)
    gy_last = call(last_kernel, [block], *arrays, weight=W_LAST)[0]
    home = moved(gy_last, last_row)
    gy_2, gy_2_last, gx_1, gx_near_own_0, gx_near_own_1, _ = together(
        gy_2, gy_2_last, gx_1, gx_near_own_0, gx_near_own_1, gy_last
    )
    for_2 = call(select_two_kernel, [block], gy_2, gy_2_last, weight=W_BACK)[0]
    back_2 = moved(for_2, in_row(2))
    gx_cut_1 = moved(gx_1, other_group)
    gx_beside_own_0 = moved(gx_near_own_0, other_core)
    gx_beside_own_1 = moved(gx_near_own_1, other_core)
    arrays = (gya_here, gyb_here, *arrays)
    gy_own = call(own_kernel, [block], *arrays)[0]
    gx_cut_0, gy_own = together(gx_cut_0, gy_own)
    parts = (gx_own_0, gx_beside_own_0, gx_cut_0)
    image_0 = call(add_three_kernel, [first], *parts, weight=W_HALF)[0]
    gx_cut_1, image_0 = together(gx_cut_1, image_0)
    parts = (gx_own_1, gx_beside_own_1, gx_cut_1)
    image_1 = call(add_three_kernel, [second], *parts, weight=W_END)[0]
    home, gy_own, image_0, image_1 = together(home, gy_own, image_0, image_1)
    gy_own = call(add_kernel, [block], gy_own, home, weight=W_HOME)[0]
    back_2, gy_own, image_0, image_1 = together(back_2, gy_own, image_0, image_1)
    return tuple(
        finish(*params, y_own, y_inv, gy_own, back_2, x_0, x_1, x_inv, image_0, image_1)
    )


def solution(mesh):
    rows = P(("cuts", "blk"), None)
    return jax.shard_map(
        local, mesh=mesh, in_specs=(rows, rows, P(), P()), out_specs=(rows, rows), check_vma=False
    )
```

```python
import jax
import jax.numpy as jnp
from jax import lax
from jax.experimental import pallas as pl
from jax.experimental.pallas import tpu as pltpu
from jax.sharding import PartitionSpec as P

GROUPS, BLOCKS, ROW = 2, 128, 8
FIRST = 64
W_ONE = 0
W_HOP = 0
W_CUT = 300_000_000
W_ARRIVE = 1000_000_000
W_FAR = 3000_000_000
W_LAST = 0
W_BACK = 0
W_HALF = 1_000_000_000
W_END = 1_000_000_000
W_HOME = 100_000_000


def moved(block, place):
    pairs = []
    for group in range(GROUPS):
        for position in range(BLOCKS):
            to_group, to_position = place(group, position)
            pairs.append((group * BLOCKS + position, to_group * BLOCKS + to_position % BLOCKS))
    return lax.ppermute(block, ("cuts", "blk"), pairs)


def next_row(group, position):
    return (group, position + ROW) if position % 2 == 0 else (1 - group, position + ROW)


def last_row(group, position):
    return (group, position - ROW) if position % 2 == 0 else (1 - group, position - ROW)


def in_row(chips):
    return lambda group, position: (
        group,
        position // ROW * ROW + (position + 2 * chips) % ROW,
    )


def other_core(group, position):
    return group, position ^ 1


def other_group(group, position):
    return 1 - group, position


def together(*values):
    return lax.optimization_barrier(values)


def split(values):
    high = values.astype(jnp.bfloat16)
    return high, (values - high.astype(jnp.float32)).astype(jnp.bfloat16)


def dot3(a, b, b_dim):
    dims = (((1,), (b_dim,)), ((), ()))
    (a_high, a_low), (b_high, b_low) = a, b

    def one(u, v):
        return lax.dot_general(u, v, dims, preferred_element_type=jnp.float32)

    return one(a_high, b_high) + (one(a_low, b_high) + one(a_high, b_low))


def places():
    position = lax.axis_index("blk")
    column = position % ROW // 2
    return position % 2 == 1, column < 2, column >= 3, column >= 1


def sigmoid(values):
    return 1.0 / (1.0 + jnp.exp(-values))


def params_kernel(log_scale, bias, out_ref):
    row_ids = lax.broadcasted_iota(jnp.int32, out_ref.shape, 0)
    scale = jnp.exp(jnp.zeros(out_ref.shape, jnp.float32) + log_scale[0])
    out_ref[...] = jnp.where(row_ids == 0, scale, bias[0])


def image_norm_kernel(_, in_ref, inverse_ref, *outs):
    normalize_kernel(in_ref, inverse_ref, *outs)


def normalize_kernel(in_ref, inverse_ref, *outs):
    values = in_ref[...]
    inverse = lax.rsqrt(jnp.sum(values * values, axis=-1, keepdims=True) + 1e-06)
    inverse_ref[...] = inverse
    values = values * inverse
    at = 0
    for out in outs:
        out[...] = values[at : at + out.shape[0], :]
        at = (at + out.shape[0]) % values.shape[0]


def split_kernel(*refs):
    *images, high_ref, low_ref = refs
    at = 0
    for image in images:
        high, low = split(image[...])
        high_ref[at : at + image.shape[0], :] = high
        low_ref[at : at + image.shape[0], :] = low
        at += image.shape[0]


def join_kernel(first_high, first_low, second_high, second_low, *refs):
    *images, high_ref, low_ref = refs
    middle = first_high.shape[0]
    at = middle + second_high.shape[0]
    high_ref[:middle, :] = first_high[...]
    low_ref[:middle, :] = first_low[...]
    high_ref[middle:at, :] = second_high[...]
    low_ref[middle:at, :] = second_low[...]
    for image in images:
        high, low = split(image[...])
        high_ref[at : at + image.shape[0], :] = high
        low_ref[at : at + image.shape[0], :] = low
        at += image.shape[0]


def far_kernel(params, *refs):
    count = (len(refs) - 3) // 2
    texts, (high_ref, low_ref, grads_ref), outs = refs[:count], refs[count:-count], refs[-count:]
    rows = texts[0].shape[0]
    image = (high_ref[...], low_ref[...])
    text = split(jnp.concatenate([ref[...] for ref in texts], axis=0))
    grads = sigmoid(params[0:1, 0:1] * dot3(text, image, 1) + params[1:2, 0:1])
    grads_ref[...] = grads
    to_text = dot3(split(grads), image, 0)
    for at, out in enumerate(outs):
        out[...] = to_text[at * rows : (at + 1) * rows, :]


def near_kernel(first, params, *refs):
    (own, last, high_ref, low_ref), outs = refs[:4], refs[4:]
    rows = own.shape[0]
    for side, grads_ref, to_text in ((0, *outs[:2]), (1, *outs[2:])):
        span = pl.ds(first + side * rows, rows)
        image = (high_ref[span, :], low_ref[span, :])
        text = own[...]
        if side == 1:
            text = jnp.where(places()[0], last[...], text)
        logits = params[0:1, 0:1] * dot3(split(text), image, 1) + params[1:2, 0:1]
        if side == 0 and first == 0:
            row_ids = lax.broadcasted_iota(jnp.int32, logits.shape, 0)
            col_ids = lax.broadcasted_iota(jnp.int32, logits.shape, 1)
            signs = jnp.where(row_ids == col_ids, -1.0, 1.0)
            grads = signs * sigmoid(signs * logits)
        else:
            grads = sigmoid(logits)
        grads_ref[...] = grads
        to_text[...] = dot3(split(grads), image, 0)


def image_kernel(first, own, last, y_1, y_3, y_2, g_here, g_near, g_13, g_2, *outs):
    rows = own.shape[0]
    far = [y_1[...], y_3[...], y_2[...]]
    here = own[...]
    near = jnp.where(places()[0], last[...], here)
    for side, text, mine in ((0, here, g_here), (1, near, g_near)):
        columns = pl.ds(first + side * rows, rows)
        grads = [g_13[:, columns], g_2[:, columns], mine[...]]
        grads = split(jnp.concatenate(grads, axis=0).T)
        to_image = dot3(grads, split(jnp.concatenate([*far, text], axis=0)), 0)
        at = 0
        for out in outs[side * len(outs) // 2 : (side + 1) * len(outs) // 2]:
            out[...] = to_image[at : at + out.shape[0], :]
            at += out.shape[0]


def select_kernel(own, last, one_ref, three_ref):
    one_ref[...] = jnp.where(places()[2], last[...], own[...])
    three_ref[...] = jnp.where(places()[3], last[...], own[...])


def select_two_kernel(two, two_last, out_ref):
    out_ref[...] = jnp.where(places()[1], two_last[...], two[...])


def last_kernel(near_a, near_b, back_1, back_3, out_ref):
    total = jnp.where(places()[0], near_a[...] + near_b[...], 0.0)
    total = total + jnp.where(places()[2], back_1[...], 0.0)
    out_ref[...] = total + jnp.where(places()[3], back_3[...], 0.0)


def own_kernel(here_a, here_b, near_a, near_b, back_1, back_3, out_ref):
    total = here_a[...] + here_b[...]
    total = total + jnp.where(places()[0], 0.0, near_a[...] + near_b[...])
    total = total + jnp.where(places()[2], 0.0, back_1[...])
    out_ref[...] = total + jnp.where(places()[3], 0.0, back_3[...])


def add_three_kernel(one, two, three, out_ref):
    out_ref[...] = one[...] + two[...] + three[...]


def copy_kernel(one, two, one_out, two_out):
    one_out[...] = one[...]
    two_out[...] = two[...]


def add_kernel(here, beside, out_ref):
    out_ref[...] = here[...] + beside[...]


def finish_kernel(params, y, y_inv, *refs):
    y_parts, x_halves, x_inv, x_totals, outs, (held, left) = (
        refs[:2],
        refs[2:4],
        refs[4],
        refs[5:7],
        refs[7:9],
        refs[9:],
    )
    copies = []
    spans = [(0, at * y.shape[0] // 2, y.shape[0] // 2) for at in (0, 1)]
    spans += [(1, 0, x_halves[0].shape[0]), (1, x_halves[0].shape[0], x_halves[1].shape[0])]
    for at, (side, first, rows) in enumerate(spans):
        span = pl.ds(first, rows)
        if side == 1:
            normal, inverse = x_halves[at - 2][...], x_inv[span, :]
            total = x_totals[at - 2][...]
        else:
            normal, inverse = y[span, :], y_inv[span, :]
            total = y_parts[0][span, :] + y_parts[1][span, :]
        total = params[0:1, 0:1] * total
        along = jnp.sum(normal * total, axis=-1, keepdims=True)
        held[side, span, :] = inverse * (total - normal * along)
        copies.append(
            pltpu.make_async_copy(
                held.at[side, span, :], outs[1 - side].at[span, :], left.at[at]
            )
        )
        copies[-1].start()
    for copy in copies:
        copy.wait()


def call(kernel, outs, *arrays, scalars=(), weight=0):
    vmem = pl.BlockSpec(memory_space=pltpu.VMEM)
    smem = pl.BlockSpec(memory_space=pltpu.SMEM)
    return pl.pallas_call(
        kernel,
        out_shape=[jax.ShapeDtypeStruct(shape, dtype) for shape, dtype in outs],
        in_specs=[smem] * len(scalars) + [vmem] * len(arrays),
        out_specs=[vmem] * len(outs),
        compiler_params=pltpu.CompilerParams(vmem_limit_bytes=16 * 2**20),
        cost_estimate=pl.CostEstimate(flops=weight, transcendentals=0, bytes_accessed=0),
    )(*scalars, *arrays)


def finish(*arrays):
    shape = arrays[1].shape
    hbm = pl.BlockSpec(memory_space=pltpu.HBM)
    return pl.pallas_call(
        finish_kernel,
        out_shape=[jax.ShapeDtypeStruct(shape, jnp.float32)] * 2,
        in_specs=[pl.BlockSpec(memory_space=pltpu.VMEM)] * len(arrays),
        out_specs=[hbm] * 2,
        scratch_shapes=[pltpu.VMEM((2, *shape), jnp.float32), pltpu.SemaphoreType.DMA((4,))],
        compiler_params=pltpu.CompilerParams(vmem_limit_bytes=16 * 2**20),
        cost_estimate=pl.CostEstimate(flops=0, transcendentals=0, bytes_accessed=0),
    )(*arrays)


def local(image_embed, text_embed, log_scale, bias):
    rows, width = image_embed.shape
    f32, bf16 = jnp.float32, jnp.bfloat16
    block = ((rows, width), f32)

    square = ((rows, rows), f32)
    pair = ((2 * rows, width), bf16)

    outs = [((rows, 1), f32), block]
    y_inv, y_own = call(normalize_kernel, outs, text_embed)
    first, second = ((FIRST, width), f32), ((rows - FIRST, width), f32)
    outs = [((rows, 1), f32), first, second]
    x_inv, x_0, x_1 = call(image_norm_kernel, outs, y_inv, image_embed)
    params = call(params_kernel, [((8, 128), f32)], scalars=(log_scale, bias))
    y_last = moved(y_own, next_row)
    y_2 = moved(y_own, in_row(2))
    x_cut_0 = moved(x_0, other_group)
    x_beside_0 = moved(x_0, other_core)
    x_beside_1 = moved(x_1, other_core)
    y_2_last = moved(y_2, next_row)
    y_last, y_own, x_0, x_1, x_beside_0, x_beside_1 = together(
        y_last, y_own, x_0, x_1, x_beside_0, x_beside_1
    )
    for_1, for_3 = call(select_kernel, [block] * 2, y_own, y_last, weight=W_ONE)
    y_1 = moved(for_1, in_row(1))
    y_3 = moved(for_3, in_row(-1))
    x_cut_0, x_1, y_own, _ = together(x_cut_0, x_1, y_own, for_1)
    xc_high, xc_low = call(
        split_kernel, [((FIRST, width), bf16)] * 2, x_cut_0, weight=W_CUT
    )
    x_1, xc_high, x_cut_0 = together(x_1, xc_high, x_cut_0)
    x_cut_1 = moved(x_1, other_group)
    x_cut_beside_0 = moved(x_cut_0, other_core)
    xa_high, xa_low = call(split_kernel, [pair] * 2, x_0, x_1, x_beside_0, x_beside_1)
    arrays = (y_own, y_last, xa_high, xa_low)
    kernel = lambda *refs: near_kernel(0, *refs)
    near = call(kernel, [square, block] * 2, *params, *arrays)
    ga_here, gya_here, ga_near, gya_near = near
    x_cut_1, x_cut_beside_0, ga_here = together(x_cut_1, x_cut_beside_0, ga_here)

    x_cut_beside_1 = moved(x_cut_1, other_core)
    images = (x_cut_1, x_cut_beside_0, x_cut_beside_1)
    outs = [((4 * rows, width), bf16)] * 2
    y_1, y_3 = call(copy_kernel, [block] * 2, y_1, y_3, weight=W_ARRIVE)
    y_1, y_3, xa_high = together(y_1, y_3, xa_high)
    x_high, x_low = call(join_kernel, outs, xa_high, xa_low, xc_high, xc_low, *images)
    outs = [((2 * rows, 4 * rows), f32)] + [block] * 2
    arrays = (*params, y_1, y_3, x_high, x_low)
    g_13, gy_1, gy_3 = call(far_kernel, outs, *arrays, weight=W_FAR)
    back_1 = moved(gy_1, in_row(-1))
    back_3 = moved(gy_3, in_row(1))
    g_13, y_2, y_2_last = together(g_13, y_2, y_2_last)
    y_2 = call(select_two_kernel, [block], y_2, y_2_last, weight=W_HOP)[0]
    outs = [((rows, 4 * rows), f32), block]
    g_2, gy_2 = call(far_kernel, outs, *params, y_2, x_high, x_low)
    gy_2_last = moved(gy_2, last_row)

    g_2, x_high = together(g_2, x_high)
    arrays = (y_own, y_last, x_high, x_low)
    kernel = lambda *refs: near_kernel(2 * rows, *refs)
    near = call(kernel, [square, block] * 2, *params, *arrays)
    gb_here, gyb_here, gb_near, gyb_near = near
    arrays = (y_own, y_last, y_1, y_3, y_2, gb_here, gb_near, g_13, g_2)
    kernel = lambda *refs: image_kernel(2 * rows, *refs)
    gx_0, gx_1, gx_near_0, gx_near_1 = call(kernel, [first, second] * 2, *arrays)
    gx_beside_0 = moved(gx_near_0, other_core)
    gx_beside_1 = moved(gx_near_1, other_core)
    gx_0 = call(add_kernel, [first], gx_0, gx_beside_0)[0]
    gx_cut_0 = moved(gx_0, other_group)
    gx_1, y_1, y_3 = together(gx_1, y_1, y_3)
    arrays = (y_own, y_last, y_1, y_3, y_2, ga_here, ga_near, g_13, g_2)
    kernel = lambda *refs: image_kernel(0, *refs)
    outs = call(kernel, [first, second] * 2, *arrays)
    gx_own_0, gx_own_1, gx_near_own_0, gx_near_own_1 = outs
    gx_1 = call(add_kernel, [second], gx_1, gx_beside_1)[0]
    back_1, back_3, gx_near_own_0, gx_near_own_1, gx_1 = together(
        back_1, back_3, gx_near_own_0, gx_near_own_1, gx_1
    )
    arrays = (gya_near, gyb_near, back_1, back_3)
    gy_last = call(last_kernel, [block], *arrays, weight=W_LAST)[0]
    home = moved(gy_last, last_row)
    gy_2, gy_2_last, gx_1, gx_near_own_0, gx_near_own_1, _ = together(
        gy_2, gy_2_last, gx_1, gx_near_own_0, gx_near_own_1, gy_last
    )
    for_2 = call(select_two_kernel, [block], gy_2, gy_2_last, weight=W_BACK)[0]
    back_2 = moved(for_2, in_row(2))
    gx_cut_1 = moved(gx_1, other_group)
    gx_beside_own_0 = moved(gx_near_own_0, other_core)
    gx_beside_own_1 = moved(gx_near_own_1, other_core)
    arrays = (gya_here, gyb_here, *arrays)
    gy_own = call(own_kernel, [block], *arrays)[0]
    gx_cut_0, gy_own = together(gx_cut_0, gy_own)
    parts = (gx_own_0, gx_beside_own_0, gx_cut_0)
    image_0 = call(add_three_kernel, [first], *parts, weight=W_HALF)[0]
    gx_cut_1, image_0 = together(gx_cut_1, image_0)
    parts = (gx_own_1, gx_beside_own_1, gx_cut_1)
    image_1 = call(add_three_kernel, [second], *parts, weight=W_END)[0]
    home, gy_own, image_0, image_1 = together(home, gy_own, image_0, image_1)
    gy_own = call(add_kernel, [block], gy_own, home, weight=W_HOME)[0]
    back_2, gy_own, image_0, image_1 = together(back_2, gy_own, image_0, image_1)
    return tuple(
        finish(*params, y_own, y_inv, gy_own, back_2, x_0, x_1, x_inv, image_0, image_1)
    )


def solution(mesh):
    rows = P(("cuts", "blk"), None)
    return jax.shard_map(
        local, mesh=mesh, in_specs=(rows, rows, P(), P()), out_specs=(rows, rows), check_vma=False
    )
```

```python
import jax
import jax.numpy as jnp
from jax import lax
from jax.experimental import pallas as pl
from jax.experimental.pallas import tpu as pltpu
from jax.sharding import PartitionSpec as P

GROUPS, BLOCKS, ROW = 2, 128, 8
FIRST = 64
W_ONE = 0
W_HOP = 0
W_CUT = 300_000_000
W_ARRIVE = 1000_000_000
W_FAR = 3000_000_000
W_LAST = 0
W_BACK = 0
W_HALF = 1_000_000_000
W_END = 1_000_000_000
W_HOME = 100_000_000


def moved(block, place):
    pairs = []
    for group in range(GROUPS):
        for position in range(BLOCKS):
            to_group, to_position = place(group, position)
            pairs.append((group * BLOCKS + position, to_group * BLOCKS + to_position % BLOCKS))
    return lax.ppermute(block, ("cuts", "blk"), pairs)


def next_row(group, position):
    return (group, position + ROW) if position % 2 == 0 else (1 - group, position + ROW)


def last_row(group, position):
    return (group, position - ROW) if position % 2 == 0 else (1 - group, position - ROW)


def in_row(chips):
    return lambda group, position: (
        group,
        position // ROW * ROW + (position + 2 * chips) % ROW,
    )


def other_core(group, position):
    return group, position ^ 1


def other_group(group, position):
    return 1 - group, position


def together(*values):
    return lax.optimization_barrier(values)


def split(values):
    high = values.astype(jnp.bfloat16)
    return high, (values - high.astype(jnp.float32)).astype(jnp.bfloat16)


def dot3(a, b, b_dim):
    dims = (((1,), (b_dim,)), ((), ()))
    (a_high, a_low), (b_high, b_low) = a, b

    def one(u, v):
        return lax.dot_general(u, v, dims, preferred_element_type=jnp.float32)

    rows = a_high.shape[0]
    both = one(jnp.concatenate([a_high, a_low], axis=0), b_high)
    return both[:rows] + (both[rows:] + one(a_high, b_low))


def places():
    position = lax.axis_index("blk")
    column = position % ROW // 2
    return position % 2 == 1, column < 2, column >= 3, column >= 1


def sigmoid(values):
    return 1.0 / (1.0 + jnp.exp(-values))


def params_kernel(log_scale, bias, out_ref):
    row_ids = lax.broadcasted_iota(jnp.int32, out_ref.shape, 0)
    scale = jnp.exp(jnp.zeros(out_ref.shape, jnp.float32) + log_scale[0])
    out_ref[...] = jnp.where(row_ids == 0, scale, bias[0])


def image_norm_kernel(_, in_ref, inverse_ref, *outs):
    normalize_kernel(in_ref, inverse_ref, *outs)


def normalize_kernel(in_ref, inverse_ref, *outs):
    values = in_ref[...]
    inverse = lax.rsqrt(jnp.sum(values * values, axis=-1, keepdims=True) + 1e-06)
    inverse_ref[...] = inverse
    values = values * inverse
    at = 0
    for out in outs:
        out[...] = values[at : at + out.shape[0], :]
        at = (at + out.shape[0]) % values.shape[0]


def split_kernel(*refs):
    *images, high_ref, low_ref = refs
    at = 0
    for image in images:
        high, low = split(image[...])
        high_ref[at : at + image.shape[0], :] = high
        low_ref[at : at + image.shape[0], :] = low
        at += image.shape[0]


def join_kernel(first_high, first_low, second_high, second_low, *refs):
    *images, high_ref, low_ref = refs
    middle = first_high.shape[0]
    at = middle + second_high.shape[0]
    high_ref[:middle, :] = first_high[...]
    low_ref[:middle, :] = first_low[...]
    high_ref[middle:at, :] = second_high[...]
    low_ref[middle:at, :] = second_low[...]
    for image in images:
        high, low = split(image[...])
        high_ref[at : at + image.shape[0], :] = high
        low_ref[at : at + image.shape[0], :] = low
        at += image.shape[0]


def far_kernel(params, *refs):
    count = (len(refs) - 3) // 2
    texts, (high_ref, low_ref, grads_ref), outs = refs[:count], refs[count:-count], refs[-count:]
    rows = texts[0].shape[0]
    image = (high_ref[...], low_ref[...])
    text = split(jnp.concatenate([ref[...] for ref in texts], axis=0))
    grads = sigmoid(params[0:1, 0:1] * dot3(text, image, 1) + params[1:2, 0:1])
    grads_ref[...] = grads
    to_text = dot3(split(grads), image, 0)
    for at, out in enumerate(outs):
        out[...] = to_text[at * rows : (at + 1) * rows, :]


def near_kernel(first, params, *refs):
    (own, last, high_ref, low_ref), outs = refs[:4], refs[4:]
    rows = own.shape[0]
    for side, grads_ref, to_text in ((0, *outs[:2]), (1, *outs[2:])):
        span = pl.ds(first + side * rows, rows)
        image = (high_ref[span, :], low_ref[span, :])
        text = own[...]
        if side == 1:
            text = jnp.where(places()[0], last[...], text)
        logits = params[0:1, 0:1] * dot3(split(text), image, 1) + params[1:2, 0:1]
        if side == 0 and first == 0:
            row_ids = lax.broadcasted_iota(jnp.int32, logits.shape, 0)
            col_ids = lax.broadcasted_iota(jnp.int32, logits.shape, 1)
            signs = jnp.where(row_ids == col_ids, -1.0, 1.0)
            grads = signs * sigmoid(signs * logits)
        else:
            grads = sigmoid(logits)
        grads_ref[...] = grads
        to_text[...] = dot3(split(grads), image, 0)


def image_kernel(first, own, last, y_1, y_3, y_2, g_here, g_near, g_13, g_2, *outs):
    rows = own.shape[0]
    far = [y_1[...], y_3[...], y_2[...]]
    here = own[...]
    near = jnp.where(places()[0], last[...], here)
    for side, text, mine in ((0, here, g_here), (1, near, g_near)):
        columns = pl.ds(first + side * rows, rows)
        grads = [g_13[:, columns], g_2[:, columns], mine[...]]
        grads = split(jnp.concatenate(grads, axis=0).T)
        to_image = dot3(grads, split(jnp.concatenate([*far, text], axis=0)), 0)
        at = 0
        for out in outs[side * len(outs) // 2 : (side + 1) * len(outs) // 2]:
            out[...] = to_image[at : at + out.shape[0], :]
            at += out.shape[0]


def select_kernel(own, last, one_ref, three_ref):
    one_ref[...] = jnp.where(places()[2], last[...], own[...])
    three_ref[...] = jnp.where(places()[3], last[...], own[...])


def select_two_kernel(two, two_last, out_ref):
    out_ref[...] = jnp.where(places()[1], two_last[...], two[...])


def last_kernel(near_a, near_b, back_1, back_3, out_ref):
    total = jnp.where(places()[0], near_a[...] + near_b[...], 0.0)
    total = total + jnp.where(places()[2], back_1[...], 0.0)
    out_ref[...] = total + jnp.where(places()[3], back_3[...], 0.0)


def own_kernel(here_a, here_b, near_a, near_b, back_1, back_3, out_ref):
    total = here_a[...] + here_b[...]
    total = total + jnp.where(places()[0], 0.0, near_a[...] + near_b[...])
    total = total + jnp.where(places()[2], 0.0, back_1[...])
    out_ref[...] = total + jnp.where(places()[3], 0.0, back_3[...])


def add_three_kernel(one, two, three, out_ref):
    out_ref[...] = one[...] + two[...] + three[...]


def copy_kernel(one, two, one_out, two_out):
    one_out[...] = one[...]
    two_out[...] = two[...]


def add_kernel(here, beside, out_ref):
    out_ref[...] = here[...] + beside[...]


def finish_kernel(params, y, y_inv, *refs):
    y_parts, x_halves, x_inv, x_totals, outs, (held, left) = (
        refs[:2],
        refs[2:4],
        refs[4],
        refs[5:7],
        refs[7:9],
        refs[9:],
    )
    copies = []
    spans = [(0, at * y.shape[0] // 2, y.shape[0] // 2) for at in (0, 1)]
    spans += [(1, 0, x_halves[0].shape[0]), (1, x_halves[0].shape[0], x_halves[1].shape[0])]
    for at, (side, first, rows) in enumerate(spans):
        span = pl.ds(first, rows)
        if side == 1:
            normal, inverse = x_halves[at - 2][...], x_inv[span, :]
            total = x_totals[at - 2][...]
        else:
            normal, inverse = y[span, :], y_inv[span, :]
            total = y_parts[0][span, :] + y_parts[1][span, :]
        total = params[0:1, 0:1] * total
        along = jnp.sum(normal * total, axis=-1, keepdims=True)
        held[side, span, :] = inverse * (total - normal * along)
        copies.append(
            pltpu.make_async_copy(
                held.at[side, span, :], outs[1 - side].at[span, :], left.at[at]
            )
        )
        copies[-1].start()
    for copy in copies:
        copy.wait()


def call(kernel, outs, *arrays, scalars=(), weight=0):
    vmem = pl.BlockSpec(memory_space=pltpu.VMEM)
    smem = pl.BlockSpec(memory_space=pltpu.SMEM)
    return pl.pallas_call(
        kernel,
        out_shape=[jax.ShapeDtypeStruct(shape, dtype) for shape, dtype in outs],
        in_specs=[smem] * len(scalars) + [vmem] * len(arrays),
        out_specs=[vmem] * len(outs),
        compiler_params=pltpu.CompilerParams(vmem_limit_bytes=16 * 2**20),
        cost_estimate=pl.CostEstimate(flops=weight, transcendentals=0, bytes_accessed=0),
    )(*scalars, *arrays)


def finish(*arrays):
    shape = arrays[1].shape
    hbm = pl.BlockSpec(memory_space=pltpu.HBM)
    return pl.pallas_call(
        finish_kernel,
        out_shape=[jax.ShapeDtypeStruct(shape, jnp.float32)] * 2,
        in_specs=[pl.BlockSpec(memory_space=pltpu.VMEM)] * len(arrays),
        out_specs=[hbm] * 2,
        scratch_shapes=[pltpu.VMEM((2, *shape), jnp.float32), pltpu.SemaphoreType.DMA((4,))],
        compiler_params=pltpu.CompilerParams(vmem_limit_bytes=16 * 2**20),
        cost_estimate=pl.CostEstimate(flops=0, transcendentals=0, bytes_accessed=0),
    )(*arrays)


def local(image_embed, text_embed, log_scale, bias):
    rows, width = image_embed.shape
    f32, bf16 = jnp.float32, jnp.bfloat16
    block = ((rows, width), f32)

    square = ((rows, rows), f32)
    pair = ((2 * rows, width), bf16)

    outs = [((rows, 1), f32), block]
    y_inv, y_own = call(normalize_kernel, outs, text_embed)
    first, second = ((FIRST, width), f32), ((rows - FIRST, width), f32)
    outs = [((rows, 1), f32), first, second]
    x_inv, x_0, x_1 = call(image_norm_kernel, outs, y_inv, image_embed)
    params = call(params_kernel, [((8, 128), f32)], scalars=(log_scale, bias))
    y_last = moved(y_own, next_row)
    y_2 = moved(y_own, in_row(2))
    x_cut_0 = moved(x_0, other_group)
    x_beside_0 = moved(x_0, other_core)
    x_beside_1 = moved(x_1, other_core)
    y_2_last = moved(y_2, next_row)
    y_last, y_own, x_0, x_1, x_beside_0, x_beside_1 = together(
        y_last, y_own, x_0, x_1, x_beside_0, x_beside_1
    )
    for_1, for_3 = call(select_kernel, [block] * 2, y_own, y_last, weight=W_ONE)
    y_1 = moved(for_1, in_row(1))
    y_3 = moved(for_3, in_row(-1))
    x_cut_0, x_1, y_own, _ = together(x_cut_0, x_1, y_own, for_1)
    xc_high, xc_low = call(
        split_kernel, [((FIRST, width), bf16)] * 2, x_cut_0, weight=W_CUT
    )
    x_1, xc_high, x_cut_0 = together(x_1, xc_high, x_cut_0)
    x_cut_1 = moved(x_1, other_group)
    x_cut_beside_0 = moved(x_cut_0, other_core)
    xa_high, xa_low = call(split_kernel, [pair] * 2, x_0, x_1, x_beside_0, x_beside_1)
    arrays = (y_own, y_last, xa_high, xa_low)
    kernel = lambda *refs: near_kernel(0, *refs)
    near = call(kernel, [square, block] * 2, *params, *arrays)
    ga_here, gya_here, ga_near, gya_near = near
    x_cut_1, x_cut_beside_0, ga_here = together(x_cut_1, x_cut_beside_0, ga_here)

    x_cut_beside_1 = moved(x_cut_1, other_core)
    images = (x_cut_1, x_cut_beside_0, x_cut_beside_1)
    outs = [((4 * rows, width), bf16)] * 2
    y_1, y_3 = call(copy_kernel, [block] * 2, y_1, y_3, weight=W_ARRIVE)
    y_1, y_3, xa_high = together(y_1, y_3, xa_high)
    x_high, x_low = call(join_kernel, outs, xa_high, xa_low, xc_high, xc_low, *images)
    outs = [((2 * rows, 4 * rows), f32)] + [block] * 2
    arrays = (*params, y_1, y_3, x_high, x_low)
    g_13, gy_1, gy_3 = call(far_kernel, outs, *arrays, weight=W_FAR)
    back_1 = moved(gy_1, in_row(-1))
    back_3 = moved(gy_3, in_row(1))
    g_13, y_2, y_2_last = together(g_13, y_2, y_2_last)
    y_2 = call(select_two_kernel, [block], y_2, y_2_last, weight=W_HOP)[0]
    outs = [((rows, 4 * rows), f32), block]
    g_2, gy_2 = call(far_kernel, outs, *params, y_2, x_high, x_low)
    gy_2_last = moved(gy_2, last_row)

    g_2, x_high = together(g_2, x_high)
    arrays = (y_own, y_last, x_high, x_low)
    kernel = lambda *refs: near_kernel(2 * rows, *refs)
    near = call(kernel, [square, block] * 2, *params, *arrays)
    gb_here, gyb_here, gb_near, gyb_near = near
    arrays = (y_own, y_last, y_1, y_3, y_2, gb_here, gb_near, g_13, g_2)
    kernel = lambda *refs: image_kernel(2 * rows, *refs)
    gx_0, gx_1, gx_near_0, gx_near_1 = call(kernel, [first, second] * 2, *arrays)
    gx_beside_0 = moved(gx_near_0, other_core)
    gx_beside_1 = moved(gx_near_1, other_core)
    gx_0 = call(add_kernel, [first], gx_0, gx_beside_0)[0]
    gx_cut_0 = moved(gx_0, other_group)
    gx_1, y_1, y_3 = together(gx_1, y_1, y_3)
    arrays = (y_own, y_last, y_1, y_3, y_2, ga_here, ga_near, g_13, g_2)
    kernel = lambda *refs: image_kernel(0, *refs)
    outs = call(kernel, [first, second] * 2, *arrays)
    gx_own_0, gx_own_1, gx_near_own_0, gx_near_own_1 = outs
    gx_1 = call(add_kernel, [second], gx_1, gx_beside_1)[0]
    back_1, back_3, gx_near_own_0, gx_near_own_1, gx_1 = together(
        back_1, back_3, gx_near_own_0, gx_near_own_1, gx_1
    )
    arrays = (gya_near, gyb_near, back_1, back_3)
    gy_last = call(last_kernel, [block], *arrays, weight=W_LAST)[0]
    home = moved(gy_last, last_row)
    gy_2, gy_2_last, gx_1, gx_near_own_0, gx_near_own_1, _ = together(
        gy_2, gy_2_last, gx_1, gx_near_own_0, gx_near_own_1, gy_last
    )
    for_2 = call(select_two_kernel, [block], gy_2, gy_2_last, weight=W_BACK)[0]
    back_2 = moved(for_2, in_row(2))
    gx_cut_1 = moved(gx_1, other_group)
    gx_beside_own_0 = moved(gx_near_own_0, other_core)
    gx_beside_own_1 = moved(gx_near_own_1, other_core)
    arrays = (gya_here, gyb_here, *arrays)
    gy_own = call(own_kernel, [block], *arrays)[0]
    gx_cut_0, gy_own = together(gx_cut_0, gy_own)
    parts = (gx_own_0, gx_beside_own_0, gx_cut_0)
    image_0 = call(add_three_kernel, [first], *parts, weight=W_HALF)[0]
    gx_cut_1, image_0 = together(gx_cut_1, image_0)
    parts = (gx_own_1, gx_beside_own_1, gx_cut_1)
    image_1 = call(add_three_kernel, [second], *parts, weight=W_END)[0]
    home, gy_own, image_0, image_1 = together(home, gy_own, image_0, image_1)
    gy_own = call(add_kernel, [block], gy_own, home, weight=W_HOME)[0]
    back_2, gy_own, image_0, image_1 = together(back_2, gy_own, image_0, image_1)
    return tuple(
        finish(*params, y_own, y_inv, gy_own, back_2, x_0, x_1, x_inv, image_0, image_1)
    )


def solution(mesh):
    rows = P(("cuts", "blk"), None)
    return jax.shard_map(
        local, mesh=mesh, in_specs=(rows, rows, P(), P()), out_specs=(rows, rows), check_vma=False
    )
```

```python
import jax
import jax.numpy as jnp
from jax import lax
from jax.experimental import pallas as pl
from jax.experimental.pallas import tpu as pltpu
from jax.sharding import PartitionSpec as P

GROUPS, BLOCKS, ROW = 2, 128, 8
FIRST = 64
MORE = 48
W_ONE = 0
W_HOP = 0
W_CUT = 300_000_000
W_ARRIVE = 1000_000_000
W_FAR = 3000_000_000
W_LAST = 0
W_BACK = 0
W_HALF = 1_000_000_000
W_END = 1_000_000_000
W_HOME = 100_000_000


def moved(block, place):
    pairs = []
    for group in range(GROUPS):
        for position in range(BLOCKS):
            to_group, to_position = place(group, position)
            pairs.append((group * BLOCKS + position, to_group * BLOCKS + to_position % BLOCKS))
    return lax.ppermute(block, ("cuts", "blk"), pairs)


def next_row(group, position):
    return (group, position + ROW) if position % 2 == 0 else (1 - group, position + ROW)


def last_row(group, position):
    return (group, position - ROW) if position % 2 == 0 else (1 - group, position - ROW)


def in_row(chips):
    return lambda group, position: (
        group,
        position // ROW * ROW + (position + 2 * chips) % ROW,
    )


def other_core(group, position):
    return group, position ^ 1


def other_group(group, position):
    return 1 - group, position


def together(*values):
    return lax.optimization_barrier(values)


def split(values):
    high = values.astype(jnp.bfloat16)
    return high, (values - high.astype(jnp.float32)).astype(jnp.bfloat16)


def dot3(a, b, b_dim):
    dims = (((1,), (b_dim,)), ((), ()))
    (a_high, a_low), (b_high, b_low) = a, b

    def one(u, v):
        return lax.dot_general(u, v, dims, preferred_element_type=jnp.float32)

    rows = a_high.shape[0]
    both = one(jnp.concatenate([a_high, a_low], axis=0), b_high)
    return both[:rows] + (both[rows:] + one(a_high, b_low))


def places():
    position = lax.axis_index("blk")
    column = position % ROW // 2
    return position % 2 == 1, column < 2, column >= 3, column >= 1


def sigmoid(values):
    return 1.0 / (1.0 + jnp.exp(-values))


def params_kernel(log_scale, bias, out_ref):
    row_ids = lax.broadcasted_iota(jnp.int32, out_ref.shape, 0)
    scale = jnp.exp(jnp.zeros(out_ref.shape, jnp.float32) + log_scale[0])
    out_ref[...] = jnp.where(row_ids == 0, scale, bias[0])


def image_norm_kernel(_, in_ref, inverse_ref, *outs):
    normalize_kernel(in_ref, inverse_ref, *outs)


def normalize_kernel(in_ref, inverse_ref, *outs):
    values = in_ref[...]
    inverse = lax.rsqrt(jnp.sum(values * values, axis=-1, keepdims=True) + 1e-06)
    inverse_ref[...] = inverse
    values = values * inverse
    at = 0
    for out in outs:
        out[...] = values[at : at + out.shape[0], :]
        at = (at + out.shape[0]) % values.shape[0]


def split_kernel(*refs):
    *images, high_ref, low_ref = refs
    at = 0
    for image in images:
        high, low = split(image[...])
        high_ref[at : at + image.shape[0], :] = high
        low_ref[at : at + image.shape[0], :] = low
        at += image.shape[0]


def join_kernel(first_high, first_low, second_high, second_low, *refs):
    *images, high_ref, low_ref = refs
    middle = first_high.shape[0]
    at = middle + second_high.shape[0]
    high_ref[:middle, :] = first_high[...]
    low_ref[:middle, :] = first_low[...]
    high_ref[middle:at, :] = second_high[...]
    low_ref[middle:at, :] = second_low[...]
    for image in images:
        high, low = split(image[...])
        high_ref[at : at + image.shape[0], :] = high
        low_ref[at : at + image.shape[0], :] = low
        at += image.shape[0]


def far_kernel(params, *refs):
    count = (len(refs) - 3) // 2
    texts, (high_ref, low_ref, grads_ref), outs = refs[:count], refs[count:-count], refs[-count:]
    rows = texts[0].shape[0]
    image = (high_ref[...], low_ref[...])
    text = split(jnp.concatenate([ref[...] for ref in texts], axis=0))
    grads = sigmoid(params[0:1, 0:1] * dot3(text, image, 1) + params[1:2, 0:1])
    grads_ref[...] = grads
    to_text = dot3(split(grads), image, 0)
    for at, out in enumerate(outs):
        out[...] = to_text[at * rows : (at + 1) * rows, :]


def near_kernel(first, params, *refs):
    (own, last, high_ref, low_ref), outs = refs[:4], refs[4:]
    rows = own.shape[0]
    for side, grads_ref, to_text in ((0, *outs[:2]), (1, *outs[2:])):
        span = pl.ds(first + side * rows, rows)
        image = (high_ref[span, :], low_ref[span, :])
        text = own[...]
        if side == 1:
            text = jnp.where(places()[0], last[...], text)
        logits = params[0:1, 0:1] * dot3(split(text), image, 1) + params[1:2, 0:1]
        if side == 0 and first == 0:
            row_ids = lax.broadcasted_iota(jnp.int32, logits.shape, 0)
            col_ids = lax.broadcasted_iota(jnp.int32, logits.shape, 1)
            signs = jnp.where(row_ids == col_ids, -1.0, 1.0)
            grads = signs * sigmoid(signs * logits)
        else:
            grads = sigmoid(logits)
        grads_ref[...] = grads
        to_text[...] = dot3(split(grads), image, 0)


def image_kernel(first, own, last, y_1, y_3, y_2, g_here, g_near, g_13, g_2, *outs):
    rows = own.shape[0]
    far = [y_1[...], y_3[...], y_2[...]]
    here = own[...]
    near = jnp.where(places()[0], last[...], here)
    for side, text, mine in ((0, here, g_here), (1, near, g_near)):
        columns = pl.ds(first + side * rows, rows)
        grads = [g_13[:, columns], g_2[:, columns], mine[...]]
        grads = split(jnp.concatenate(grads, axis=0).T)
        to_image = dot3(grads, split(jnp.concatenate([*far, text], axis=0)), 0)
        at = 0
        for out in outs[side * len(outs) // 2 : (side + 1) * len(outs) // 2]:
            out[...] = to_image[at : at + out.shape[0], :]
            at += out.shape[0]


def select_kernel(own, last, one_ref, three_ref):
    one_ref[...] = jnp.where(places()[2], last[...], own[...])
    three_ref[...] = jnp.where(places()[3], last[...], own[...])


def select_two_kernel(two, two_last, out_ref):
    out_ref[...] = jnp.where(places()[1], two_last[...], two[...])


def last_kernel(near_a, near_b, back_1, back_3, out_ref):
    total = jnp.where(places()[0], near_a[...] + near_b[...], 0.0)
    total = total + jnp.where(places()[2], back_1[...], 0.0)
    out_ref[...] = total + jnp.where(places()[3], back_3[...], 0.0)


def own_kernel(here_a, here_b, near_a, near_b, back_1, back_3, out_ref):
    total = here_a[...] + here_b[...]
    total = total + jnp.where(places()[0], 0.0, near_a[...] + near_b[...])
    total = total + jnp.where(places()[2], 0.0, back_1[...])
    out_ref[...] = total + jnp.where(places()[3], 0.0, back_3[...])


def add_three_kernel(one, two, three, out_ref):
    out_ref[...] = one[...] + two[...] + three[...]


def copy_kernel(one, two, one_out, two_out):
    one_out[...] = one[...]
    two_out[...] = two[...]


def add_kernel(here, beside, out_ref):
    out_ref[...] = here[...] + beside[...]


def finish_kernel(params, y, y_inv, *refs):
    y_parts, x_halves, x_inv, x_totals, outs, (held, left) = (
        refs[:2],
        refs[2:4],
        refs[4],
        refs[5:7],
        refs[7:9],
        refs[9:],
    )
    copies = []
    spans = [(0, at * y.shape[0] // 2, y.shape[0] // 2) for at in (0, 1)]
    spans += [(1, 0, x_halves[0].shape[0]), (1, x_halves[0].shape[0], x_halves[1].shape[0])]
    for at, (side, first, rows) in enumerate(spans):
        span = pl.ds(first, rows)
        if side == 1:
            normal, inverse = x_halves[at - 2][...], x_inv[span, :]
            total = x_totals[at - 2][...]
        else:
            normal, inverse = y[span, :], y_inv[span, :]
            total = y_parts[0][span, :] + y_parts[1][span, :]
        total = params[0:1, 0:1] * total
        along = jnp.sum(normal * total, axis=-1, keepdims=True)
        held[side, span, :] = inverse * (total - normal * along)
        copies.append(
            pltpu.make_async_copy(
                held.at[side, span, :], outs[1 - side].at[span, :], left.at[at]
            )
        )
        copies[-1].start()
    for copy in copies:
        copy.wait()


def call(kernel, outs, *arrays, scalars=(), weight=0):
    vmem = pl.BlockSpec(memory_space=pltpu.VMEM)
    smem = pl.BlockSpec(memory_space=pltpu.SMEM)
    return pl.pallas_call(
        kernel,
        out_shape=[jax.ShapeDtypeStruct(shape, dtype) for shape, dtype in outs],
        in_specs=[smem] * len(scalars) + [vmem] * len(arrays),
        out_specs=[vmem] * len(outs),
        compiler_params=pltpu.CompilerParams(vmem_limit_bytes=16 * 2**20),
        cost_estimate=pl.CostEstimate(flops=weight, transcendentals=0, bytes_accessed=0),
    )(*scalars, *arrays)


def finish(*arrays):
    shape = arrays[1].shape
    hbm = pl.BlockSpec(memory_space=pltpu.HBM)
    return pl.pallas_call(
        finish_kernel,
        out_shape=[jax.ShapeDtypeStruct(shape, jnp.float32)] * 2,
        in_specs=[pl.BlockSpec(memory_space=pltpu.VMEM)] * len(arrays),
        out_specs=[hbm] * 2,
        scratch_shapes=[pltpu.VMEM((2, *shape), jnp.float32), pltpu.SemaphoreType.DMA((4,))],
        compiler_params=pltpu.CompilerParams(vmem_limit_bytes=16 * 2**20),
        cost_estimate=pl.CostEstimate(flops=0, transcendentals=0, bytes_accessed=0),
    )(*arrays)


def local(image_embed, text_embed, log_scale, bias):
    rows, width = image_embed.shape
    f32, bf16 = jnp.float32, jnp.bfloat16
    block = ((rows, width), f32)

    square = ((rows, rows), f32)
    pair = ((2 * rows, width), bf16)

    outs = [((rows, 1), f32), block]
    y_inv, y_own = call(normalize_kernel, outs, text_embed)
    first, second = ((FIRST, width), f32), ((rows - FIRST, width), f32)
    more, less = ((MORE, width), f32), ((rows - MORE, width), f32)
    outs = [((rows, 1), f32), first, second, more, less]
    x_inv, x_0, x_1, x_more, x_less = call(image_norm_kernel, outs, y_inv, image_embed)
    params = call(params_kernel, [((8, 128), f32)], scalars=(log_scale, bias))
    y_last = moved(y_own, next_row)
    y_2 = moved(y_own, in_row(2))
    x_cut_0 = moved(x_0, other_group)
    x_beside_0 = moved(x_0, other_core)
    x_beside_1 = moved(x_1, other_core)
    y_2_last = moved(y_2, next_row)
    y_last, y_own, x_0, x_1, x_beside_0, x_beside_1 = together(
        y_last, y_own, x_0, x_1, x_beside_0, x_beside_1
    )
    for_1, for_3 = call(select_kernel, [block] * 2, y_own, y_last, weight=W_ONE)
    y_1 = moved(for_1, in_row(1))
    y_3 = moved(for_3, in_row(-1))
    x_cut_0, x_1, y_own, _ = together(x_cut_0, x_1, y_own, for_1)
    xc_high, xc_low = call(
        split_kernel, [((FIRST, width), bf16)] * 2, x_cut_0, weight=W_CUT
    )
    x_1, xc_high, x_cut_0 = together(x_1, xc_high, x_cut_0)
    x_cut_1 = moved(x_1, other_group)
    x_cut_beside_0 = moved(x_cut_0, other_core)
    xa_high, xa_low = call(split_kernel, [pair] * 2, x_0, x_1, x_beside_0, x_beside_1)
    arrays = (y_own, y_last, xa_high, xa_low)
    kernel = lambda *refs: near_kernel(0, *refs)
    near = call(kernel, [square, block] * 2, *params, *arrays)
    ga_here, gya_here, ga_near, gya_near = near
    x_cut_1, x_cut_beside_0, ga_here = together(x_cut_1, x_cut_beside_0, ga_here)

    x_cut_beside_1 = moved(x_cut_1, other_core)
    images = (x_cut_1, x_cut_beside_0, x_cut_beside_1)
    outs = [((4 * rows, width), bf16)] * 2
    y_1, y_3 = call(copy_kernel, [block] * 2, y_1, y_3, weight=W_ARRIVE)
    y_1, y_3, xa_high = together(y_1, y_3, xa_high)
    x_high, x_low = call(join_kernel, outs, xa_high, xa_low, xc_high, xc_low, *images)
    outs = [((2 * rows, 4 * rows), f32)] + [block] * 2
    arrays = (*params, y_1, y_3, x_high, x_low)
    g_13, gy_1, gy_3 = call(far_kernel, outs, *arrays, weight=W_FAR)
    back_1 = moved(gy_1, in_row(-1))
    back_3 = moved(gy_3, in_row(1))
    g_13, y_2, y_2_last = together(g_13, y_2, y_2_last)
    y_2 = call(select_two_kernel, [block], y_2, y_2_last, weight=W_HOP)[0]
    outs = [((rows, 4 * rows), f32), block]
    g_2, gy_2 = call(far_kernel, outs, *params, y_2, x_high, x_low)
    gy_2_last = moved(gy_2, last_row)

    g_2, x_high = together(g_2, x_high)
    arrays = (y_own, y_last, x_high, x_low)
    kernel = lambda *refs: near_kernel(2 * rows, *refs)
    near = call(kernel, [square, block] * 2, *params, *arrays)
    gb_here, gyb_here, gb_near, gyb_near = near
    arrays = (y_own, y_last, y_1, y_3, y_2, gb_here, gb_near, g_13, g_2)
    kernel = lambda *refs: image_kernel(2 * rows, *refs)
    gx_0, gx_1, gx_near_0, gx_near_1 = call(kernel, [more, less] * 2, *arrays)
    gx_beside_0 = moved(gx_near_0, other_core)
    gx_beside_1 = moved(gx_near_1, other_core)
    gx_0 = call(add_kernel, [more], gx_0, gx_beside_0)[0]
    gx_cut_0 = moved(gx_0, other_group)
    gx_1, y_1, y_3 = together(gx_1, y_1, y_3)
    arrays = (y_own, y_last, y_1, y_3, y_2, ga_here, ga_near, g_13, g_2)
    kernel = lambda *refs: image_kernel(0, *refs)
    outs = call(kernel, [more, less] * 2, *arrays)
    gx_own_0, gx_own_1, gx_near_own_0, gx_near_own_1 = outs
    gx_1 = call(add_kernel, [less], gx_1, gx_beside_1)[0]
    back_1, back_3, gx_near_own_0, gx_near_own_1, gx_1 = together(
        back_1, back_3, gx_near_own_0, gx_near_own_1, gx_1
    )
    arrays = (gya_near, gyb_near, back_1, back_3)
    gy_last = call(last_kernel, [block], *arrays, weight=W_LAST)[0]
    home = moved(gy_last, last_row)
    gy_2, gy_2_last, gx_1, gx_near_own_0, gx_near_own_1, _ = together(
        gy_2, gy_2_last, gx_1, gx_near_own_0, gx_near_own_1, gy_last
    )
    for_2 = call(select_two_kernel, [block], gy_2, gy_2_last, weight=W_BACK)[0]
    back_2 = moved(for_2, in_row(2))
    gx_cut_1 = moved(gx_1, other_group)
    gx_beside_own_0 = moved(gx_near_own_0, other_core)
    gx_beside_own_1 = moved(gx_near_own_1, other_core)
    arrays = (gya_here, gyb_here, *arrays)
    gy_own = call(own_kernel, [block], *arrays)[0]
    gx_cut_0, gy_own = together(gx_cut_0, gy_own)
    parts = (gx_own_0, gx_beside_own_0, gx_cut_0)
    image_0 = call(add_three_kernel, [more], *parts, weight=W_HALF)[0]
    gx_cut_1, image_0 = together(gx_cut_1, image_0)
    parts = (gx_own_1, gx_beside_own_1, gx_cut_1)
    image_1 = call(add_three_kernel, [less], *parts, weight=W_END)[0]
    home, gy_own, image_0, image_1 = together(home, gy_own, image_0, image_1)
    gy_own = call(add_kernel, [block], gy_own, home, weight=W_HOME)[0]
    back_2, gy_own, image_0, image_1 = together(back_2, gy_own, image_0, image_1)
    return tuple(
        finish(*params, y_own, y_inv, gy_own, back_2, x_more, x_less, x_inv, image_0, image_1)
    )


def solution(mesh):
    rows = P(("cuts", "blk"), None)
    return jax.shard_map(
        local, mesh=mesh, in_specs=(rows, rows, P(), P()), out_specs=(rows, rows), check_vma=False
    )
```
